256 devices in a mesh: aa: 16 (over x_lo, y, core), ba: 16 (over x_hi, z).
Axes of the slice: x: 4 (x_hi: 2, x_lo: 2; x = x_hi * 2 + x_lo), y: 4, z: 8, core: 2. Of those that a mesh axis runs over, the one named last changes fastest.
Arguments:
- pair_amplitude: bfloat16 [1024, 1024, 5, 128], P('aa', 'ba'), may hold values from -0.5 to 0.5
- row_amplitude: bfloat16 [1024, 2, 5, 128], P(('aa', 'ba')), may hold values from -0.5 to 0.5
- column_amplitude: bfloat16 [1024, 2, 5, 128], P(('ba', 'aa')), may hold values from -0.5 to 0.5
- row_integral: bfloat16 [1024, 3200], P(('aa', 'ba')), may hold values from -6 to 6
- column_integral: bfloat16 [1024, 3200], P(('ba', 'aa')), may hold values from -6 to 6
- step_integral: bfloat16 [2, 3200], replicated, may hold values from -6 to 6
- virtual_energy: float32 [1024], replicated, may hold values from 0.3 to 2
- occupied_energy: float32 [5], replicated, may hold values from -1.5 to -0.2
- step_energy: float32 [2], replicated, may hold values from 0.3 to 2
Outputs:
- row_residual: float32 [1024, 2, 5, 128], P(('aa', 'ba'))
- column_residual: float32 [1024, 2, 5, 128], P(('ba', 'aa'))
The draws below stay inside these ranges and needn't reach their ends.
All inputs are finite; a program needn't handle non-finite values.
Results may differ from the reference program's by a relative error of at most 0.0005.
Values may be sent and summed in bfloat16 or wider, within the bound.
A program may use at most 64 MiB of HBM per device.

```python
import math
import jax
import jax.numpy as jnp
from jax import lax

NV = 1024
NO = 128
OT = 5
NC = 2


def steps_of(key, dims, split, low, high):
    gain, own = 1.0, jax.random.fold_in(key, 6)
    for axis_at, shards_of in split:
        heights = jnp.exp(jax.random.uniform(jax.random.fold_in(own, axis_at), (shards_of,), jnp.float32, low / len(split), high / len(split)))
        gain = gain * jnp.repeat(heights, dims[axis_at] // shards_of).reshape([-1 if axis == axis_at else 1 for axis in range(len(dims))])
    return gain


def gaussian(key, shape, scale, limit, split=(), held_as=jnp.bfloat16):
    gain = steps_of(key, shape, split, -0.22, 0.18) if split else 1.0
    entries = jax.random.normal(key, shape, jnp.float32) * scale * gain
    return jnp.minimum(jnp.maximum(entries, -limit), limit).astype(held_as)


def setup_inputs(seed: int = 0) -> dict:
    splits = jax.random.split(jax.random.key(seed), 10)
    pair_amplitude = gaussian(splits[0], (NV, NV, OT, NO), NO ** -0.5, 0.5, ((0, 16), (1, 16)))
    row_amplitude = gaussian(splits[1], (NV, NC, OT, NO), NO ** -0.5, 0.5, ((0, 256),))
    column_amplitude = gaussian(splits[2], (NV, NC, OT, NO), NO ** -0.5, 0.5, ((0, 256),))
    row_integral = gaussian(splits[3], (NV, NO * OT * OT), 1.0, 6.0, ((0, 256),))
    column_integral = gaussian(splits[4], (NV, NO * OT * OT), 1.0, 6.0, ((0, 256),))
    step_integral = gaussian(splits[5], (NC, NO * OT * OT), 1.0, 6.0)
    virtual_energy = jnp.clip(jax.random.uniform(splits[6], (NV,), jnp.float32, 0.3, 2.0), 0.3, 2.0)
    occupied_energy = jnp.clip(jax.random.uniform(splits[7], (OT,), jnp.float32, -1.5, -0.2), -1.5, -0.2)
    step_energy = jnp.clip(jax.random.uniform(splits[8], (NC,), jnp.float32, 0.3, 2.0), 0.3, 2.0)
    return dict(pair_amplitude=pair_amplitude, row_amplitude=row_amplitude, column_amplitude=column_amplitude, row_integral=row_integral, column_integral=column_integral, step_integral=step_integral, virtual_energy=virtual_energy, occupied_energy=occupied_energy, step_energy=step_energy)


def block_terms(pair_block, lead_step, lead_table, tail_step, tail_table, table, lead_energy, tail_energy, energy_c, occupied_sum):
    triples = jnp.einsum('abil,ljk->abijk', pair_block, table)
    triples = triples + jnp.einsum('abjl,lki->abijk', pair_block, table)
    triples = triples + jnp.einsum('ail,bljk->abijk', lead_step, tail_table)
    triples = triples + jnp.einsum('akl,blij->abijk', lead_step, tail_table)
    triples = triples + jnp.einsum('bjl,alki->abijk', tail_step, lead_table)
    triples = triples + jnp.einsum('bkl,alij->abijk', tail_step, lead_table)
    denominator = lead_energy[:, None, None, None, None] + tail_energy[None, :, None, None, None] + energy_c - occupied_sum[None, None]
    weighted = lax.optimization_barrier((triples / denominator).astype(jnp.bfloat16)).astype(jnp.float32)
    row_part = jnp.einsum('abijk,bljk->ail', weighted, tail_table)
    column_part = jnp.einsum('abijk,alki->bjl', weighted, lead_table)
    return (row_part, column_part)

def reference(pair_amplitude, row_amplitude, column_amplitude, row_integral, column_integral, step_integral, virtual_energy, occupied_energy, step_energy):
    block = min(64, NV)
    factor = 1.0 / (math.sqrt(NV) * OT)
    occupied_sum = occupied_energy[:, None, None] + occupied_energy[None, :, None] + occupied_energy[None, None, :]
    step_table = step_integral.reshape(NC, NO, OT, OT).astype(jnp.float32)
    lead_all = row_integral.reshape(NV, NO, OT, OT)
    tail_table = column_integral.reshape(NV, NO, OT, OT).astype(jnp.float32)
    row_steps = []
    column_steps = []
    for which in range(NC):
        tail_step = column_amplitude[:, which].astype(jnp.float32)
        lead_source = row_amplitude[:, which]

        def one_block(column_total, index):
            start = (index * block).astype(jnp.int32)
            pair_block = lax.dynamic_slice_in_dim(pair_amplitude, start, block, 0).astype(jnp.float32)
            lead_step = lax.dynamic_slice_in_dim(lead_source, start, block, 0).astype(jnp.float32)
            lead_table = lax.dynamic_slice_in_dim(lead_all, start, block, 0).astype(jnp.float32)
            lead_energy = lax.dynamic_slice_in_dim(virtual_energy, start, block, 0)
            row_part, column_part = block_terms(pair_block, lead_step, lead_table, tail_step, tail_table, step_table[which], lead_energy, virtual_energy, step_energy[which], occupied_sum)
            return (column_total + column_part, row_part)
        column_total, row_parts = lax.scan(one_block, jnp.zeros((NV, OT, NO), jnp.float32), jnp.arange(NV // block, dtype=jnp.int32))
        row_steps.append(row_parts.reshape(NV, OT, NO))
        column_steps.append(column_total)
    row_residual = jnp.stack(row_steps, 1) * factor
    column_residual = jnp.stack(column_steps, 1) * factor
    return (row_residual, column_residual)
```

```python
import functools
import math

import jax
import jax.numpy as jnp
from jax import lax
from jax.experimental import pallas as pl
from jax.experimental.pallas import tpu as pltpu
from jax.sharding import PartitionSpec as P

F32 = jnp.float32
BF16 = jnp.bfloat16
MESH = pl.DeviceIdType.MESH
GROUP = 16
OWN = 4
OT = 5
JK = OT * OT
NC = 2
SI = OT * NC
NO = 128
CHUNK = 144
PART = 40
AROWS = 56
NT = (((1,), (1,)), ((), ()))


def dot_nt(x, y):
    return lax.dot_general(x, y, NT, preferred_element_type=F32)


def split_l(g_ref, h_ref, q_ref, r_ref, u_ref, row_chunk, col_chunk, q_out, amp):
    top = jnp.concatenate([g_ref[...].astype(F32), h_ref[...].astype(F32)], 0)
    low = jnp.concatenate(
        [q_ref[...].astype(F32), jnp.zeros((6, JK * NO), F32)], 0
    )
    row = lax.broadcasted_iota(jnp.int32, (NO, NO), 0)
    col = lax.broadcasted_iota(jnp.int32, (NO, NO), 1)
    perm = (row == ((JK * col) & 127)).astype(F32).astype(BF16)
    stacked = jnp.concatenate(
        [
            part[:, m * NO : (m + 1) * NO]
            for m in range(JK)
            for part in (top, low)
        ],
        0,
    ).astype(BF16)
    moved = jnp.dot(stacked, perm, preferred_element_type=F32)
    lane = lax.broadcasted_iota(jnp.int32, (8, NO), 1)
    tops, lows = [], []
    for jk in range(JK):
        source = (JK * ((lane - 41 * jk) & 127) + jk) >> 7
        t = moved[0:8]
        w = moved[8:16]
        for m in range(1, JK):
            mask = source == m
            t = jnp.where(mask, moved[16 * m : 16 * m + 8], t)
            w = jnp.where(mask, moved[16 * m + 8 : 16 * m + 16], w)
        shift = (-41 * jk) % 128
        if shift:
            t = pltpu.roll(t, shift, 1)
            w = pltpu.roll(w, shift, 1)
        tops.append(t)
        lows.append(w)
    for which, (src, dst) in enumerate(((r_ref, row_chunk), (u_ref, col_chunk))):
        amp[...] = src[...].astype(F32)
        pieces = [t[4 * which : 4 * which + 4] for t in tops]
        pieces += [amp[pl.ds(c, OWN, stride=SI), :] for c in range(SI)]
        pieces.append(jnp.zeros((4, NO), F32))
        for k in range(9):
            dst[16 * k : 16 * k + 16, :] = jnp.concatenate(
                pieces[4 * k : 4 * k + 4], 0
            ).astype(BF16)
    rows = [lows[jk][s : s + 1] for s in range(NC) for jk in range(JK)]
    rows.append(jnp.zeros((64 - NC * JK, NO), F32))
    q_out[...] = jnp.concatenate(rows, 0).astype(BF16)


def gather_body(
    g_ref, h_ref, q_ref, r_ref, u_ref, rows_ref, cols_ref, q_out,
    row_chunk, col_chunk, amp, send_sems, row_sems, col_sems, own_sems,
):
    me_a = lax.axis_index("aa")
    me_b = lax.axis_index("ba")
    barrier = pltpu.get_barrier_semaphore()
    for step in range(1, GROUP):
        pl.semaphore_signal(
            barrier, inc=1, device_id=(me_a, lax.rem(me_b + step, GROUP)),
            device_id_type=MESH,
        )
        pl.semaphore_signal(
            barrier, inc=1, device_id=(lax.rem(me_a + step, GROUP), me_b),
            device_id_type=MESH,
        )
    split_l(g_ref, h_ref, q_ref, r_ref, u_ref, row_chunk, col_chunk, q_out, amp)
    pl.semaphore_wait(barrier, 2 * (GROUP - 1))
    copies = []
    for step in range(1, GROUP):
        for which, (src, dst, sems, at, target) in enumerate(
            (
                (row_chunk, rows_ref, row_sems, me_b, (me_a, lax.rem(me_b + step, GROUP))),
                (col_chunk, cols_ref, col_sems, me_a, (lax.rem(me_a + step, GROUP), me_b)),
            )
        ):
            copy = pltpu.make_async_remote_copy(
                src_ref=src,
                dst_ref=dst.at[pl.ds(at * CHUNK, CHUNK), :],
                send_sem=send_sems.at[which, step],
                recv_sem=sems.at[step],
                device_id=target,
                device_id_type=MESH,
            )
            copy.start()
            copies.append(copy)
    own = [
        pltpu.make_async_copy(
            row_chunk, rows_ref.at[pl.ds(me_b * CHUNK, CHUNK), :], own_sems.at[0]
        ),
        pltpu.make_async_copy(
            col_chunk, cols_ref.at[pl.ds(me_a * CHUNK, CHUNK), :], own_sems.at[1]
        ),
    ]
    for copy in own:
        copy.start()
    for copy in own:
        copy.wait()
    for copy in copies:
        copy.wait()


def spread(src, wide, kind):
    for k in range(9):
        blocks = [
            src[e * CHUNK + 16 * k : e * CHUNK + 16 * k + 16, :].astype(F32)
            for e in range(GROUP)
        ]
        for c in range(4):
            at = 4 * k + c
            if at >= JK + SI:
                continue
            tile = jnp.concatenate([b[4 * c : 4 * c + 4] for b in blocks], 0)
            wide(at, tile.astype(BF16))


def compute_a(t_ref, q_ref, a_out):
    q = q_ref[0:AROWS, :]

    def pair(n, _):
        for i in range(OT):
            block = jnp.concatenate(
                [
                    t_ref[2 * n, i], t_ref[2 * n + 32, i],
                    t_ref[2 * n + 1, i], t_ref[2 * n + 33, i],
                ],
                0,
            )
            part = dot_nt(q, block)
            for half in range(2):
                at = pl.multiple_of((2 * n + half) * (OT * AROWS) + i * AROWS, 8)
                a_out[pl.ds(at, AROWS), :] = part[:, half * NO : (half + 1) * NO]
        return 0

    lax.fori_loop(0, 16, pair, 0)


def put_rows(g2, r2, at, tile):
    dst, c = (g2, at) if at < JK else (r2, at - JK)
    dst[c * 32 : c * 32 + 32, 0:NO] = tile[0:32]
    dst[c * 32 : c * 32 + 32, NO : 2 * NO] = tile[32:64]


def put_cols(bdh, bdu, at, tile):
    dst, c = (bdh, at) if at < JK else (bdu, at - JK)
    dst[c * NO : c * NO + 64, 0:NO] = tile
    dst[c * NO + 64 : c * NO + NO, NO : 2 * NO] = tile


def clear_off(bdh, bdu):
    zero = jnp.zeros((64, NO), BF16)
    for dst, count in ((bdh, JK), (bdu, SI)):
        for c in range(count):
            dst[c * NO : c * NO + 64, NO : 2 * NO] = zero
            dst[c * NO + 64 : c * NO + NO, 0:NO] = zero


def pair_energy(ve_ref, me_a, me_b):
    lane = lax.broadcasted_iota(jnp.int32, (32, NO), 1)
    row = lax.broadcasted_iota(jnp.int32, (32, NO), 0)
    lead = jnp.broadcast_to(ve_ref[pl.ds(me_a // 2, 1), :], (32, NO))
    first = lax.rem(me_a, 2) * 64
    halves = [
        jnp.sum(
            jnp.where(lane == first + 32 * half + row, lead, 0.0), 1, keepdims=True
        )
        for half in range(2)
    ]
    tail = ve_ref[pl.ds(me_b // 2, 1), :]
    turned = pltpu.roll(jnp.broadcast_to(tail, (8, NO)), 64, 1)[0:1]
    lane1 = lane[0:1]
    keep = (lane1 // 64) == lax.rem(me_b, 2)
    tail = jnp.where(keep, tail, turned)
    return jnp.where(lane < 64, halves[0], halves[1]) + tail


def compute_pc(g2, r2, bdh, bdu, p_out, c_out):
    r = r2[...]

    for n in range(JK // 2 + 1):
        width = 2 if n < JK // 2 else 1
        part = dot_nt(r, bdh[2 * n * NO : (2 * n + width) * NO, :])
        for half in range(width):
            p_out[(2 * n + half) * 320 : (2 * n + half + 1) * 320, :] = part[
                :, half * NO : (half + 1) * NO
            ]
    for n in range(OT):
        for m in range(5):
            part = dot_nt(
                g2[m * 160 : (m + 1) * 160, :], bdu[2 * n * NO : (2 * n + 2) * NO, :]
            )
            for half in range(2):
                at = (2 * n + half) * 800 + m * 160
                c_out[at : at + 160, :] = part[:, half * NO : (half + 1) * NO]


def weigh(oe_ref, se_ref, base, a_in, p_in, c_in, yr, yc):
    def one(n, _):
        i = n // NC
        s = lax.rem(n, NC)
        start = base + se_ref[s]
        for j in range(OT):
            for k in range(OT):
                jk = j * OT + k
                ki = k * OT + i
                ij = i * OT + j
                energy = (oe_ref[i] + oe_ref[j]) + oe_ref[k]
                tiles = []
                for v in range(4):
                    first = v * 8 * OT * AROWS + s * JK
                    w = a_in[pl.ds(first + i * AROWS + jk, 8, stride=OT * AROWS), :]
                    w = w + a_in[pl.ds(first + j * AROWS + ki, 8, stride=OT * AROWS), :]
                    at = pl.multiple_of(jk * 320 + (i * NC + s) * 32 + v * 8, 8)
                    w = w + p_in[pl.ds(at, 8), :]
                    at = pl.multiple_of(ij * 320 + (k * NC + s) * 32 + v * 8, 8)
                    w = w + p_in[pl.ds(at, 8), :]
                    at = pl.multiple_of((j * NC + s) * 800 + ki * 32 + v * 8, 8)
                    w = w + c_in[pl.ds(at, 8), :]
                    at = pl.multiple_of((k * NC + s) * 800 + ij * 32 + v * 8, 8)
                    w = w + c_in[pl.ds(at, 8), :]
                    tiles.append(w / (start[v * 8 : v * 8 + 8] - energy))
                y = jnp.concatenate(tiles, 0).astype(BF16)
                at = pl.multiple_of((i * NC + s) * 32, 32)
                yr[pl.ds(at, 32), jk * NO : (jk + 1) * NO] = y
                at = pl.multiple_of((j * NC + s) * 800 + ki * 32, 32)
                yc[pl.ds(at, 32), :] = y
        return 0

    lax.fori_loop(0, SI, one, 0)


def residuals(g2, bdh, yr, yc, res, row_out, col_out):
    out = jnp.dot(yr[...], bdh[...], preferred_element_type=F32)
    for c in range(SI):
        for half in range(2):
            res[c * 64 + half * 32 : c * 64 + half * 32 + 32, :] = out[
                c * 32 : c * 32 + 32, half * NO : (half + 1) * NO
            ]
    for c in range(SI):
        for v in range(OWN):
            row_out[pl.ds(v * SI + c, GROUP, stride=PART), :] = res[
                pl.ds(c * 64 + v, GROUP, stride=OWN), :
            ]
    turned = g2[...].T
    lane = lax.broadcasted_iota(jnp.int32, (NO, NO), 1)
    for n in range(OT):
        wide = jnp.concatenate(
            [yc[(2 * n + half) * 800 : (2 * n + half + 1) * 800, :] for half in range(2)], 1
        )
        out = jnp.dot(turned, wide, preferred_element_type=F32)
        for half in range(2):
            piece = out[:, half * NO : (half + 1) * NO]
            both = jnp.where(lane < 64, piece[0:NO], piece[NO:]).T
            at = (2 * n + half) * 64
            res[at : at + 64, :] = both[0:64] + both[64:128]
    for c in range(SI):
        for v in range(OWN):
            col_out[pl.ds(v * SI + c, GROUP, stride=PART), :] = res[
                pl.ds(c * 64 + v, GROUP, stride=OWN), :
            ]


def compute_body(
    t_hbm, q_ref, rows_ref, cols_ref, ve_ref, oe_ref, se_ref, row_out, col_out,
    t_ref, a_ref, g2, r2, bdh, bdu, p_ref, c_ref, yr, yc, res, t_sem,
):
    copy = pltpu.make_async_copy(t_hbm, t_ref, t_sem)
    copy.start()
    clear_off(bdh, bdu)
    spread(rows_ref, functools.partial(put_rows, g2, r2), 0)
    spread(cols_ref, functools.partial(put_cols, bdh, bdu), 1)
    compute_pc(g2, r2, bdh, bdu, p_ref, c_ref)
    copy.wait()
    compute_a(t_ref, q_ref, a_ref)
    base = pair_energy(ve_ref, lax.axis_index("aa"), lax.axis_index("ba"))
    weigh(oe_ref, se_ref, base, a_ref, p_ref, c_ref, yr, yc)
    residuals(g2, bdh, yr, yc, res, row_out, col_out)


def compute_call(t, q, rows, cols, ve, oe, se):
    vm = pl.BlockSpec(memory_space=pltpu.VMEM)
    sm = pl.BlockSpec(memory_space=pltpu.SMEM)
    shape = jax.ShapeDtypeStruct((GROUP * PART, NO), F32)
    return pl.pallas_call(
        compute_body,
        out_shape=(shape, shape),
        in_specs=[pl.BlockSpec(memory_space=pl.ANY), vm, vm, vm, vm, sm, sm],
        out_specs=(vm, vm),
        scratch_shapes=[
            pltpu.VMEM((64, OT, 64, NO), BF16),
            pltpu.VMEM((32 * OT * AROWS, NO), F32),
            pltpu.VMEM((JK * 32, 2 * NO), BF16),
            pltpu.VMEM((SI * 32, 2 * NO), BF16),
            pltpu.VMEM((JK * NO, 2 * NO), BF16),
            pltpu.VMEM((SI * NO, 2 * NO), BF16),
            pltpu.VMEM((JK * 320, NO), F32),
            pltpu.VMEM((SI * 800, NO), F32),
            pltpu.VMEM((320, JK * NO), BF16),
            pltpu.VMEM((SI * 800, NO), BF16),
            pltpu.VMEM((SI * 64, NO), F32),
            pltpu.SemaphoreType.DMA,
        ],
        compiler_params=pltpu.CompilerParams(vmem_limit_bytes=48 * 2**20),
    )(t, q, rows, cols, ve, oe, se)


def scatter_body(
    factor, row_ref, col_ref, row_out, col_out, row_in, col_in, send_sems, row_sems, col_sems
):
    me_a = lax.axis_index("aa")
    me_b = lax.axis_index("ba")
    barrier = pltpu.get_barrier_semaphore()
    for step in range(1, GROUP):
        pl.semaphore_signal(
            barrier, inc=1, device_id=(me_a, lax.rem(me_b + step, GROUP)),
            device_id_type=MESH,
        )
        pl.semaphore_signal(
            barrier, inc=1, device_id=(lax.rem(me_a + step, GROUP), me_b),
            device_id_type=MESH,
        )
    pl.semaphore_wait(barrier, 2 * (GROUP - 1))
    copies = []
    for step in range(1, GROUP):
        to_b = lax.rem(me_b + step, GROUP)
        to_a = lax.rem(me_a + step, GROUP)
        for which, (src, dst, sems, at, target) in enumerate(
            (
                (row_ref, row_in, row_sems, to_b, (me_a, to_b)),
                (col_ref, col_in, col_sems, to_a, (to_a, me_b)),
            )
        ):
            copy = pltpu.make_async_remote_copy(
                src_ref=src.at[pl.ds(at * PART, PART), :],
                dst_ref=dst.at[step],
                send_sem=send_sems.at[which, step],
                recv_sem=sems.at[step],
                device_id=target,
                device_id_type=MESH,
            )
            copy.start()
            copies.append(copy)
    row_sum = row_ref[pl.ds(me_b * PART, PART), :]
    col_sum = col_ref[pl.ds(me_a * PART, PART), :]
    for n, copy in enumerate(copies):
        copy.wait_recv()
        if n % 2 == 0:
            row_sum = row_sum + row_in[n // 2 + 1]
        else:
            col_sum = col_sum + col_in[n // 2 + 1]
    row_out[...] = row_sum * factor
    col_out[...] = col_sum * factor
    for copy in copies:
        copy.wait_send()


def on_device(
    pair_amplitude,
    row_amplitude,
    column_amplitude,
    row_integral,
    column_integral,
    step_integral,
    virtual_energy,
    occupied_energy,
    step_energy,
):
    vm = pl.BlockSpec(memory_space=pltpu.VMEM)
    factor = 1.0 / (math.sqrt(virtual_energy.shape[0]) * OT)
    t = pair_amplitude.transpose(0, 2, 1, 3)
    r = row_amplitude.transpose(0, 2, 1, 3).reshape(PART, NO)
    u = column_amplitude.transpose(0, 2, 1, 3).reshape(PART, NO)
    whole = jax.ShapeDtypeStruct((GROUP * CHUNK, NO), BF16)
    rows, cols, q = pl.pallas_call(
        gather_body,
        out_shape=(whole, whole, jax.ShapeDtypeStruct((64, NO), BF16)),
        in_specs=[vm] * 5,
        out_specs=(vm, vm, vm),
        scratch_shapes=[
            pltpu.VMEM((CHUNK, NO), BF16),
            pltpu.VMEM((CHUNK, NO), BF16),
            pltpu.VMEM((PART, NO), F32),
            pltpu.SemaphoreType.DMA((2, GROUP)),
            pltpu.SemaphoreType.DMA((GROUP,)),
            pltpu.SemaphoreType.DMA((GROUP,)),
            pltpu.SemaphoreType.DMA((2,)),
        ],
        compiler_params=pltpu.CompilerParams(
            collective_id=0, has_side_effects=True, vmem_limit_bytes=32 * 2**20
        ),
    )(row_integral, column_integral, step_integral, r, u)
    row_part, col_part = compute_call(
        t, q, rows, cols, virtual_energy.reshape(8, NO), occupied_energy, step_energy
    )
    part = jax.ShapeDtypeStruct((PART, NO), F32)
    row_res, col_res = pl.pallas_call(
        functools.partial(scatter_body, factor),
        out_shape=(part, part),
        in_specs=[vm] * 2,
        out_specs=(vm, vm),
        scratch_shapes=[
            pltpu.VMEM((GROUP, PART, NO), F32),
            pltpu.VMEM((GROUP, PART, NO), F32),
            pltpu.SemaphoreType.DMA((2, GROUP)),
            pltpu.SemaphoreType.DMA((GROUP,)),
            pltpu.SemaphoreType.DMA((GROUP,)),
        ],
        compiler_params=pltpu.CompilerParams(
            collective_id=1, has_side_effects=True, vmem_limit_bytes=32 * 2**20
        ),
    )(row_part, col_part)
    return tuple(
        x.reshape(OWN, OT, NC, NO).transpose(0, 2, 1, 3) for x in (row_res, col_res)
    )


def solution(mesh):
    placed = (
        P("aa", "ba", None, None),
        P(("aa", "ba"), None, None, None),
        P(("ba", "aa"), None, None, None),
        P(("aa", "ba"), None),
        P(("ba", "aa"), None),
        P(),
        P(),
        P(),
        P(),
    )
    return jax.shard_map(
        on_device,
        mesh=mesh,
        in_specs=placed,
        out_specs=(P(("aa", "ba"), None, None, None), P(("ba", "aa"), None, None, None)),
        check_vma=False,
    )
```

```python
import functools
import math

import jax
import jax.numpy as jnp
from jax import lax
from jax.experimental import pallas as pl
from jax.experimental.pallas import tpu as pltpu
from jax.sharding import PartitionSpec as P

F32 = jnp.float32
BF16 = jnp.bfloat16
MESH = pl.DeviceIdType.MESH
GROUP = 16
OWN = 4
OT = 5
JK = OT * OT
NC = 2
SI = OT * NC
NO = 128
CHUNK = 144
PART = 24
USED = OWN * OT
AROWS = 56
NT = (((1,), (1,)), ((), ()))


def dot_nt(x, y):
    return lax.dot_general(x, y, NT, preferred_element_type=F32)


def split_l(g_ref, h_ref, q_ref, r_ref, u_ref, row_chunk, col_chunk, q_out, amp):
    top = jnp.concatenate([g_ref[...].astype(F32), h_ref[...].astype(F32)], 0)
    low = jnp.concatenate(
        [q_ref[...].astype(F32), jnp.zeros((6, JK * NO), F32)], 0
    )
    row = lax.broadcasted_iota(jnp.int32, (NO, NO), 0)
    col = lax.broadcasted_iota(jnp.int32, (NO, NO), 1)
    perm = (row == ((JK * col) & 127)).astype(F32).astype(BF16)
    stacked = jnp.concatenate(
        [
            part[:, m * NO : (m + 1) * NO]
            for m in range(JK)
            for part in (top, low)
        ],
        0,
    ).astype(BF16)
    moved = jnp.dot(stacked, perm, preferred_element_type=F32)
    lane = lax.broadcasted_iota(jnp.int32, (8, NO), 1)
    tops, lows = [], []
    for jk in range(JK):
        source = (JK * ((lane - 41 * jk) & 127) + jk) >> 7
        t = moved[0:8]
        w = moved[8:16]
        for m in range(1, JK):
            mask = source == m
            t = jnp.where(mask, moved[16 * m : 16 * m + 8], t)
            w = jnp.where(mask, moved[16 * m + 8 : 16 * m + 16], w)
        shift = (-41 * jk) % 128
        if shift:
            t = pltpu.roll(t, shift, 1)
            w = pltpu.roll(w, shift, 1)
        tops.append(t)
        lows.append(w)
    for which, (src, dst) in enumerate(((r_ref, row_chunk), (u_ref, col_chunk))):
        amp[...] = src[...].astype(F32)
        pieces = [t[4 * which : 4 * which + 4] for t in tops]
        pieces += [
            amp[pl.ds(i * NC + s, OWN, stride=SI), :]
            for s in range(NC)
            for i in range(OT)
        ]
        pieces.append(jnp.zeros((4, NO), F32))
        for k in range(9):
            dst[16 * k : 16 * k + 16, :] = jnp.concatenate(
                pieces[4 * k : 4 * k + 4], 0
            ).astype(BF16)
    rows = [lows[jk][s : s + 1] for s in range(NC) for jk in range(JK)]
    rows.append(jnp.zeros((64 - NC * JK, NO), F32))
    q_out[...] = jnp.concatenate(rows, 0).astype(BF16)


class Place:
    def __init__(self):
        self.a = lax.axis_index("aa")
        self.b = lax.axis_index("ba")
        self.core = lax.rem(self.a, 2)
        self.y = lax.rem(self.a // 2, 4)
        self.xl = self.a // 8
        self.xh = self.b // 8
        self.z = lax.rem(self.b, 8)

    def index_b(self, q, k):
        xh = 1 - self.xh if q else self.xh
        return xh * 8 + lax.rem(self.z - k + 8, 8)

    def along_b(self, q, k):
        return (self.a, self.index_b(q, k))

    def index_a(self, q, d, c):
        xl = 1 - self.xl if q else self.xl
        core = 1 - self.core if c else self.core
        return (xl * 4 + lax.rem(self.y - d + 4, 4)) * 2 + core

    def along_a(self, q, d, c):
        return (self.index_a(q, d, c), self.b)


def compute_a(here, t_ref, q_ref, a_out, first, count):
    q = q_ref[0:AROWS, :]

    def pair(n, _):
        at_k = n // 2
        v = 2 * lax.rem(n, 2)
        zk = lax.rem(here.z - at_k + 8, 8)
        near = (here.xh * 8 + zk) * OWN + v
        far = ((1 - here.xh) * 8 + zk) * OWN + v
        for i in range(OT):
            block = jnp.concatenate(
                [t_ref[near, i], t_ref[far, i], t_ref[near + 1, i], t_ref[far + 1, i]], 0
            )
            part = dot_nt(q, block)
            for half in range(2):
                at = pl.multiple_of((2 * n + half) * (OT * AROWS) + i * AROWS, 8)
                a_out[pl.ds(at, AROWS), :] = part[:, half * NO : (half + 1) * NO]
        return 0

    lax.fori_loop(first, first + count, pair, 0)


def pair_energy(here, ve_ref):
    lane = lax.broadcasted_iota(jnp.int32, (32, NO), 1)
    row = lax.broadcasted_iota(jnp.int32, (32, NO), 0)
    zk = (here.z - (row >> 2)) & 7
    lead = jnp.broadcast_to(ve_ref[pl.ds(here.a // 2, 1), :], (32, NO))
    first = lax.rem(here.a, 2) * 64
    halves = []
    for xh in (here.xh, 1 - here.xh):
        at = first + (xh * 8 + zk) * OWN + (row & 3)
        halves.append(jnp.sum(jnp.where(lane == at, lead, 0.0), 1, keepdims=True))
    tail = ve_ref[pl.ds(here.b // 2, 1), :]
    turned = pltpu.roll(jnp.broadcast_to(tail, (8, NO)), 64, 1)[0:1]
    keep = (lane[0:1] // 64) == lax.rem(here.b, 2)
    tail = jnp.where(keep, tail, turned)
    return jnp.where(lane < 64, halves[0], halves[1]) + tail


def spread(src, wide):
    for k in range(9):
        blocks = [
            src[e * CHUNK + 16 * k : e * CHUNK + 16 * k + 16, :].astype(F32)
            for e in range(GROUP)
        ]
        for c in range(4):
            at = 4 * k + c
            if at >= JK + SI:
                continue
            tile = jnp.concatenate([b[4 * c : 4 * c + 4] for b in blocks], 0)
            wide(at, tile.astype(BF16))


def put_rows(g2, r2, at, tile):
    dst, c = (g2, at) if at < JK else (r2, at - JK)
    dst[c * 32 : c * 32 + 32, 0:NO] = tile[0:32]
    dst[c * 32 : c * 32 + 32, NO : 2 * NO] = tile[32:64]


def put_cols(bdh, bdu, at, tile):
    dst, c = (bdh, at) if at < JK else (bdu, at - JK)
    dst[c * NO : c * NO + 64, 0:NO] = tile
    dst[c * NO + 64 : c * NO + NO, NO : 2 * NO] = tile


def clear_off(bdh, bdu):
    zero = jnp.zeros((64, NO), BF16)
    for dst, count in ((bdh, JK), (bdu, SI)):
        for c in range(count):
            dst[c * NO : c * NO + 64, NO : 2 * NO] = zero
            dst[c * NO + 64 : c * NO + NO, 0:NO] = zero


def compute_pc(g2, r2, bdh, bdu, p_out, c_out):
    r = r2[...]

    for n in range(JK // 2 + 1):
        width = 2 if n < JK // 2 else 1
        part = dot_nt(r, bdh[2 * n * NO : (2 * n + width) * NO, :])
        for half in range(width):
            p_out[(2 * n + half) * 320 : (2 * n + half + 1) * 320, :] = part[
                :, half * NO : (half + 1) * NO
            ]
    for n in range(OT):
        for m in range(5):
            part = dot_nt(
                g2[m * 160 : (m + 1) * 160, :], bdu[2 * n * NO : (2 * n + 2) * NO, :]
            )
            for half in range(2):
                at = (2 * n + half) * 800 + m * 160
                c_out[at : at + 160, :] = part[:, half * NO : (half + 1) * NO]


def weigh(oe_ref, se_ref, base, s, a_in, p_in, c_in, yr, yc):
    start = base + se_ref[s]

    def one(i, _):
        for j in range(OT):
            for k in range(OT):
                jk = j * OT + k
                ki = k * OT + i
                ij = i * OT + j
                energy = (oe_ref[i] + oe_ref[j]) + oe_ref[k]
                tiles = []
                for v in range(4):
                    first = v * 8 * OT * AROWS + s * JK
                    w = a_in[pl.ds(first + i * AROWS + jk, 8, stride=OT * AROWS), :]
                    w = w + a_in[pl.ds(first + j * AROWS + ki, 8, stride=OT * AROWS), :]
                    at = pl.multiple_of(jk * 320 + (s * OT + i) * 32 + v * 8, 8)
                    w = w + p_in[pl.ds(at, 8), :]
                    at = pl.multiple_of(ij * 320 + (s * OT + k) * 32 + v * 8, 8)
                    w = w + p_in[pl.ds(at, 8), :]
                    at = pl.multiple_of((s * OT + j) * 800 + ki * 32 + v * 8, 8)
                    w = w + c_in[pl.ds(at, 8), :]
                    at = pl.multiple_of((s * OT + k) * 800 + ij * 32 + v * 8, 8)
                    w = w + c_in[pl.ds(at, 8), :]
                    tiles.append(w / (start[v * 8 : v * 8 + 8] - energy))
                y = jnp.concatenate(tiles, 0).astype(BF16)
                at = pl.multiple_of((s * OT + i) * 32, 32)
                yr[pl.ds(at, 32), jk * NO : (jk + 1) * NO] = y
                at = pl.multiple_of((s * OT + j) * 800 + ki * 32, 32)
                yc[pl.ds(at, 32), :] = y
        return 0

    lax.fori_loop(0, OT, one, 0)


def deal(res, out):
    for i in range(OT):
        for v in range(OWN):
            out[pl.ds(v * OT + i, GROUP, stride=PART), :] = res[
                pl.ds(i * 64 + v, GROUP, stride=OWN), :
            ]


def row_residual(s, bdh, yr, res, row_out):
    out = jnp.dot(yr[s * 160 : (s + 1) * 160, :], bdh[...], preferred_element_type=F32)
    for i in range(OT):
        for half in range(2):
            res[i * 64 + half * 32 : i * 64 + half * 32 + 32, :] = out[
                i * 32 : i * 32 + 32, half * NO : (half + 1) * NO
            ]
    deal(res, row_out)


def col_residual(s, turned, yc, res, col_out):
    lane = lax.broadcasted_iota(jnp.int32, (NO, NO), 1)
    wide = jnp.concatenate(
        [yc[(s * OT + j) * 800 : (s * OT + j + 1) * 800, :] for j in range(OT)], 1
    )
    out = jnp.dot(turned[...], wide, preferred_element_type=F32)
    for j in range(OT):
        piece = out[:, j * NO : (j + 1) * NO]
        both = jnp.where(lane < 64, piece[0:NO], piece[NO:]).T
        res[j * 64 : j * 64 + 64, :] = both[0:64] + both[64:128]
    deal(res, col_out)


class Gather:
    def __init__(self, here, rows, cols, send_sems, row_sems, col_sems):
        self.here, self.rows, self.cols = here, rows, cols
        self.send_sems, self.row_sems, self.col_sems = send_sems, row_sems, col_sems
        self.sent = []

    def copy(self, src, dst, recv_sem, target):
        copy = pltpu.make_async_remote_copy(
            src_ref=src,
            dst_ref=dst,
            send_sem=self.send_sems.at[len(self.sent)],
            recv_sem=recv_sem,
            device_id=target,
            device_id_type=MESH,
        )
        copy.start()
        self.sent.append(copy)

    def row_slot(self, q, k):
        at = (q * 8 + k) * CHUNK
        return self.rows.at[at : at + CHUNK, :]

    def col_slot(self, q, d, c):
        at = pl.multiple_of(self.here.index_a(q, d, c) * CHUNK, 16)
        return self.cols.at[pl.ds(at, CHUNK), :]

    def swap_row(self):
        self.copy(
            self.row_slot(0, 0), self.row_slot(1, 0), self.row_sems.at[1, 0],
            self.here.along_b(1, 0),
        )

    def up(self, q, k):
        self.copy(
            self.row_slot(q, k), self.row_slot(q, k + 1), self.row_sems.at[q, k + 1],
            self.here.along_b(0, -1),
        )

    def down(self, q, k):
        to = (k + 7) % 8
        self.copy(
            self.row_slot(q, k), self.row_slot(q, to), self.row_sems.at[q, to],
            self.here.along_b(0, 1),
        )

    def got_row(self, q, k):
        pltpu.make_async_remote_copy(
            src_ref=self.row_slot(q, k), dst_ref=self.row_slot(q, k),
            send_sem=self.row_sems.at[q, k], recv_sem=self.row_sems.at[q, k],
            device_id=self.here.along_b(0, 1), device_id_type=MESH,
        ).wait_recv()

    def col_to(self, q, d, c, kind, step, target):
        slot = self.col_slot(q, d, c)
        self.copy(slot, slot, self.col_sems.at[kind, step], target)

    def swap_col(self):
        self.col_to(0, 0, 0, 1, 0, self.here.along_a(1, 0, 0))

    def round_col(self, q):
        for d in range(1, 4):
            self.col_to(q, 0, 0, q, d, self.here.along_a(0, -d, 0))

    def twin_col(self, q, d):
        self.col_to(q, d, 0, 2 + q, d, self.here.along_a(0, 0, 1))

    def got_col(self, kind, d):
        slot = self.col_slot(kind % 2, d, kind // 2)
        pltpu.make_async_remote_copy(
            src_ref=slot, dst_ref=slot,
            send_sem=self.col_sems.at[kind, d], recv_sem=self.col_sems.at[kind, d],
            device_id=self.here.along_b(0, 1), device_id_type=MESH,
        ).wait_recv()


def scatter(here, s, along_rows, part, into, send_sems, recv_sems):
    copies = []
    for n in range(1, GROUP):
        if along_rows:
            target = here.along_b(n // 8, n % 8)
            at = n * PART
        else:
            target = here.along_a(n // 8, n // 2 % 4, n % 2)
            at = pl.multiple_of(target[0] * PART, 8)
        copy = pltpu.make_async_remote_copy(
            src_ref=part.at[s, pl.ds(at, PART), :],
            dst_ref=into.at[s, n * PART : (n + 1) * PART, :],
            send_sem=send_sems.at[s, n],
            recv_sem=recv_sems.at[s, n],
            device_id=target,
            device_id_type=MESH,
        )
        copy.start()
        copies.append(copy)
    return copies


def whole_body(
    factor,
    t_hbm, g_hbm, h_hbm, q_hbm, r_hbm, u_hbm, ve_hbm, oe_hbm, se_hbm,
    row_out, col_out,
    t_ref, g_in, h_in, q_in, r_in, u_in, ve_ref, oe_ref, se_ref,
    q_ref, amp, rows, cols, a_ref, g2, r2, bdh, bdu, p_ref, c_ref, yr, yc, turned, res,
    row_part, col_part, row_into, col_into, last,
    in_sems, gather_sems, row_sems, col_sems, out_row_sems, out_col_sems, sum_row_sems,
    sum_col_sems,
):
    here = Place()
    loads = [
        pltpu.make_async_copy(src, dst, in_sems.at[n])
        for n, (src, dst) in enumerate(
            (
                (g_hbm, g_in), (h_hbm, h_in), (q_hbm, q_in), (r_hbm, r_in), (u_hbm, u_in),
                (ve_hbm, ve_ref), (oe_hbm, oe_ref), (se_hbm, se_ref), (t_hbm, t_ref),
            )
        )
    ]
    for load in loads:
        load.start()
    barrier = pltpu.get_barrier_semaphore()
    near = [here.along_b(0, 1), here.along_b(0, 7), here.along_b(1, 0)]
    near += [here.along_a(0, d, 0) for d in range(1, 4)]
    near += [here.along_a(1, 0, 0), here.along_a(0, 0, 1)]
    for target in near:
        pl.semaphore_signal(barrier, inc=1, device_id=target, device_id_type=MESH)
    for load in loads[:5]:
        load.wait()
    own_col = cols.at[pl.ds(pl.multiple_of(here.a * CHUNK, 16), CHUNK), :]
    split_l(
        g_in, h_in, q_in, r_in, u_in, rows.at[0:CHUNK, :], own_col, q_ref, amp
    )
    pl.semaphore_wait(barrier, len(near))
    net = Gather(here, rows, cols, gather_sems, row_sems, col_sems)
    net.swap_row()
    net.up(0, 0)
    net.down(0, 0)
    net.swap_col()
    net.round_col(0)
    net.twin_col(0, 0)
    clear_off(bdh, bdu)
    for load in loads[5:]:
        load.wait()
    compute_a(here, t_ref, q_ref, a_ref, 0, 2)
    net.got_row(0, 1)
    net.up(0, 1)
    net.got_row(0, 7)
    net.down(0, 7)
    net.got_row(1, 0)
    net.up(1, 0)
    net.down(1, 0)
    net.got_col(1, 0)
    net.round_col(1)
    net.twin_col(1, 0)
    compute_a(here, t_ref, q_ref, a_ref, 2, 3)
    net.got_row(0, 2)
    net.up(0, 2)
    net.got_row(0, 6)
    net.down(0, 6)
    for d in range(1, 4):
        net.got_col(0, d)
        net.twin_col(0, d)
    compute_a(here, t_ref, q_ref, a_ref, 5, 3)
    net.got_row(1, 1)
    net.up(1, 1)
    net.got_row(1, 7)
    net.down(1, 7)
    for d in range(1, 4):
        net.got_col(1, d)
        net.twin_col(1, d)
    compute_a(here, t_ref, q_ref, a_ref, 8, 3)
    net.got_row(0, 3)
    net.up(0, 3)
    net.got_row(0, 5)
    compute_a(here, t_ref, q_ref, a_ref, 11, 3)
    net.got_row(1, 2)
    net.up(1, 2)
    net.got_row(1, 6)
    net.down(1, 6)
    compute_a(here, t_ref, q_ref, a_ref, 14, 2)
    net.got_row(1, 3)
    net.got_row(1, 5)
    net.down(1, 5)
    for kind in (2, 3):
        for d in range(4):
            net.got_col(kind, d)
    spread(cols, functools.partial(put_cols, bdh, bdu))
    base = pair_energy(here, ve_ref)
    net.got_row(0, 4)
    net.got_row(1, 4)
    spread(rows, functools.partial(put_rows, g2, r2))
    for copy in net.sent:
        copy.wait_send()
    compute_pc(g2, r2, bdh, bdu, p_ref, c_ref)
    turned[...] = g2[...].T
    sums = [[], []]
    for s in range(NC):
        weigh(oe_ref, se_ref, base, s, a_ref, p_ref, c_ref, yr, yc)
        row_residual(s, bdh, yr, res, row_part.at[s])
        sums[0] += scatter(here, s, True, row_part, row_into, out_row_sems, sum_row_sems)
    for s in range(NC):
        col_residual(s, turned, yc, res, col_part.at[s])
        sums[1] += scatter(here, s, False, col_part, col_into, out_col_sems, sum_col_sems)
    for which, (part, into, out, own) in enumerate(
        (
            (col_part, col_into, col_out, pl.multiple_of(here.a * PART, 8)),
            (row_part, row_into, row_out, 0),
        )
    ):
        for s in range(NC):
            total = part[s, pl.ds(own, PART), :]
            for n in range(1, GROUP):
                sums[1 - which][s * (GROUP - 1) + n - 1].wait_recv()
                total = total + into[s, n * PART : (n + 1) * PART, :]
            last[pl.ds(s, PART, stride=NC), :] = total * factor
        out[...] = last[0 : NC * USED, :]
    for copy in sums[0] + sums[1]:
        copy.wait_send()


def on_device(
    pair_amplitude,
    row_amplitude,
    column_amplitude,
    row_integral,
    column_integral,
    step_integral,
    virtual_energy,
    occupied_energy,
    step_energy,
):
    factor = 1.0 / (math.sqrt(virtual_energy.shape[0]) * OT)
    t = pair_amplitude.transpose(0, 2, 1, 3)
    r = row_amplitude.transpose(0, 2, 1, 3).reshape(OWN * SI, NO)
    u = column_amplitude.transpose(0, 2, 1, 3).reshape(OWN * SI, NO)
    ve = virtual_energy.reshape(8, NO)
    operands = (
        t, row_integral, column_integral, step_integral, r, u, ve, occupied_energy, step_energy
    )
    out = jax.ShapeDtypeStruct((NC * USED, NO), F32)
    vm = pl.BlockSpec(memory_space=pltpu.VMEM)
    spaces = [pltpu.VMEM] * 7 + [pltpu.SMEM] * 2
    order = (0, 1, 2, 3, 4, 5, 6, 7, 8)
    dma = pltpu.SemaphoreType.DMA
    results = pl.pallas_call(
        functools.partial(whole_body, factor),
        out_shape=(out, out),
        in_specs=[pl.BlockSpec(memory_space=pl.ANY)] * 9,
        out_specs=(vm, vm),
        scratch_shapes=[spaces[n](operands[n].shape, operands[n].dtype) for n in order]
        + [
            pltpu.VMEM((64, NO), BF16),
            pltpu.VMEM((OWN * SI, NO), F32),
            pltpu.VMEM((GROUP * CHUNK, NO), BF16),
            pltpu.VMEM((GROUP * CHUNK, NO), BF16),
            pltpu.VMEM((32 * OT * AROWS, NO), F32),
            pltpu.VMEM((JK * 32, 2 * NO), BF16),
            pltpu.VMEM((SI * 32, 2 * NO), BF16),
            pltpu.VMEM((JK * NO, 2 * NO), BF16),
            pltpu.VMEM((SI * NO, 2 * NO), BF16),
            pltpu.VMEM((JK * 320, NO), F32),
            pltpu.VMEM((SI * 800, NO), F32),
            pltpu.VMEM((320, JK * NO), BF16),
            pltpu.VMEM((SI * 800, NO), BF16),
            pltpu.VMEM((2 * NO, 800), BF16),
            pltpu.VMEM((OT * 64, NO), F32),
            pltpu.VMEM((NC, GROUP * PART, NO), F32),
            pltpu.VMEM((NC, GROUP * PART, NO), F32),
            pltpu.VMEM((NC, GROUP * PART, NO), F32),
            pltpu.VMEM((NC, GROUP * PART, NO), F32),
            pltpu.VMEM((NC * PART, NO), F32),
            dma((9,)),
            dma((30,)),
            dma((2, 8)),
            dma((4, 4)),
            dma((NC, GROUP)),
            dma((NC, GROUP)),
            dma((NC, GROUP)),
            dma((NC, GROUP)),
        ],
        compiler_params=pltpu.CompilerParams(
            collective_id=0, has_side_effects=True, vmem_limit_bytes=56 * 2**20
        ),
    )(*operands)
    return tuple(
        x.reshape(OWN, OT, NC, NO).transpose(0, 2, 1, 3) for x in results
    )


def solution(mesh):
    placed = (
        P("aa", "ba", None, None),
        P(("aa", "ba"), None, None, None),
        P(("ba", "aa"), None, None, None),
        P(("aa", "ba"), None),
        P(("ba", "aa"), None),
        P(),
        P(),
        P(),
        P(),
    )
    return jax.shard_map(
        on_device,
        mesh=mesh,
        in_specs=placed,
        out_specs=(P(("aa", "ba"), None, None, None), P(("ba", "aa"), None, None, None)),
        check_vma=False,
    )
```

```python
import functools
import math

import jax
import jax.numpy as jnp
from jax import lax
from jax.experimental import pallas as pl
from jax.experimental.pallas import tpu as pltpu
from jax.sharding import PartitionSpec as P

F32 = jnp.float32
BF16 = jnp.bfloat16
MESH = pl.DeviceIdType.MESH
GROUP = 16
OWN = 4
OT = 5
JK = OT * OT
NC = 2
SI = OT * NC
NO = 128
CHUNK = 144
PART = 24
USED = OWN * OT
ORDER = (1, 7, 2, 6, 3, 5, 4)
AROWS = 56
NT = (((1,), (1,)), ((), ()))


def dot_nt(x, y):
    return lax.dot_general(x, y, NT, preferred_element_type=F32)


def by_jk(moved, first, stride, count):
    lane = lax.broadcasted_iota(jnp.int32, (8, NO), 1)
    found = []
    for jk in range(JK):
        source = (JK * ((lane - 41 * jk) & 127) + jk) >> 7
        t = moved[first : first + 8]
        for m in range(1, JK):
            at = first + stride * m
            t = jnp.where(source == m, moved[at : at + 8], t)
        shift = (-41 * jk) % 128
        found.append(pltpu.roll(t, shift, 1) if shift else t)
    return found


def permute_lanes(parts):
    row = lax.broadcasted_iota(jnp.int32, (NO, NO), 0)
    col = lax.broadcasted_iota(jnp.int32, (NO, NO), 1)
    perm = (row == ((JK * col) & 127)).astype(F32).astype(BF16)
    stacked = jnp.concatenate(
        [part[:, m * NO : (m + 1) * NO] for m in range(JK) for part in parts], 0
    ).astype(BF16)
    return jnp.dot(stacked, perm, preferred_element_type=F32)


def put_chunk(tables, src, amp, dst):
    amp[...] = src[...].astype(F32)
    pieces = tables + [
        amp[pl.ds(i * NC + s, OWN, stride=SI), :] for s in range(NC) for i in range(OT)
    ]
    pieces.append(jnp.zeros((4, NO), F32))
    for k in range(9):
        dst[16 * k : 16 * k + 16, :] = jnp.concatenate(
            pieces[4 * k : 4 * k + 4], 0
        ).astype(BF16)


def split_q(q_ref, q_out):
    low = jnp.concatenate([q_ref[...].astype(F32), jnp.zeros((6, JK * NO), F32)], 0)
    lows = by_jk(permute_lanes([low]), 0, 8, JK)
    rows = [lows[jk][s : s + 1] for s in range(NC) for jk in range(JK)]
    rows.append(jnp.zeros((64 - NC * JK, NO), F32))
    q_out[...] = jnp.concatenate(rows, 0).astype(BF16)


def split_l(g_ref, h_ref, r_ref, u_ref, row_chunk, col_chunk, amp):
    top = jnp.concatenate([g_ref[...].astype(F32), h_ref[...].astype(F32)], 0)
    tops = by_jk(permute_lanes([top]), 0, 8, JK)
    put_chunk([t[0:4] for t in tops], r_ref, amp.at[0], row_chunk)
    put_chunk([t[4:8] for t in tops], u_ref, amp.at[1], col_chunk)


class Place:
    def __init__(self):
        self.a = lax.axis_index("aa")
        self.b = lax.axis_index("ba")
        self.core = lax.rem(self.a, 2)
        self.y = lax.rem(self.a // 2, 4)
        self.xl = self.a // 8
        self.xh = self.b // 8
        self.z = lax.rem(self.b, 8)

    def index_b(self, q, k):
        xh = 1 - self.xh if q else self.xh
        return xh * 8 + lax.rem(self.z - k + 8, 8)

    def along_b(self, q, k):
        return (self.a, self.index_b(q, k))

    def index_a(self, q, d, c):
        xl = 1 - self.xl if q else self.xl
        core = 1 - self.core if c else self.core
        return (xl * 4 + lax.rem(self.y - d + 4, 4)) * 2 + core

    def along_a(self, q, d, c):
        return (self.index_a(q, d, c), self.b)


def compute_a(here, t_ref, q_ref, a_out, first, count):
    q = q_ref[0:AROWS, :]

    def pair(n, _):
        at_k = n // 2
        v = 2 * lax.rem(n, 2)
        zk = lax.rem(here.z - at_k + 8, 8)
        near = (here.xh * 8 + zk) * OWN + v
        far = ((1 - here.xh) * 8 + zk) * OWN + v
        for i in range(OT):
            block = jnp.concatenate(
                [t_ref[near, i], t_ref[far, i], t_ref[near + 1, i], t_ref[far + 1, i]], 0
            )
            part = dot_nt(q, block)
            for half in range(2):
                at = pl.multiple_of((2 * n + half) * (OT * AROWS) + i * AROWS, 8)
                a_out[pl.ds(at, AROWS), :] = part[:, half * NO : (half + 1) * NO]
        return 0

    lax.fori_loop(first, first + count, pair, 0)


def pair_energy(here, ve_ref):
    lane = lax.broadcasted_iota(jnp.int32, (32, NO), 1)
    row = lax.broadcasted_iota(jnp.int32, (32, NO), 0)
    zk = (here.z - (row >> 2)) & 7
    lead = jnp.broadcast_to(ve_ref[pl.ds(here.a // 2, 1), :], (32, NO))
    first = lax.rem(here.a, 2) * 64
    halves = []
    for xh in (here.xh, 1 - here.xh):
        at = first + (xh * 8 + zk) * OWN + (row & 3)
        halves.append(jnp.sum(jnp.where(lane == at, lead, 0.0), 1, keepdims=True))
    tail = ve_ref[pl.ds(here.b // 2, 1), :]
    turned = pltpu.roll(jnp.broadcast_to(tail, (8, NO)), 64, 1)[0:1]
    keep = (lane[0:1] // 64) == lax.rem(here.b, 2)
    tail = jnp.where(keep, tail, turned)
    return jnp.where(lane < 64, halves[0], halves[1]) + tail


def spread(src, wide):
    for k in range(9):
        blocks = [
            src[e * CHUNK + 16 * k : e * CHUNK + 16 * k + 16, :].astype(F32)
            for e in range(GROUP)
        ]
        for c in range(4):
            at = 4 * k + c
            if at >= JK + SI:
                continue
            tile = jnp.concatenate([b[4 * c : 4 * c + 4] for b in blocks], 0)
            wide(at, tile.astype(BF16))


def put_rows(g2, r2, at, tile):
    dst, c = (g2, at) if at < JK else (r2, at - JK)
    dst[c * 32 : c * 32 + 32, 0:NO] = tile[0:32]
    dst[c * 32 : c * 32 + 32, NO : 2 * NO] = tile[32:64]


def put_cols(bdh, bdu, at, tile):
    dst, c = (bdh, at) if at < JK else (bdu, at - JK)
    dst[c * NO : c * NO + 64, 0:NO] = tile
    dst[c * NO + 64 : c * NO + NO, NO : 2 * NO] = tile


def clear_off(bdh, bdu):
    zero = jnp.zeros((64, NO), BF16)
    for dst, count in ((bdh, JK), (bdu, SI)):
        for c in range(count):
            dst[c * NO : c * NO + 64, NO : 2 * NO] = zero
            dst[c * NO + 64 : c * NO + NO, 0:NO] = zero


def compute_pc(g2, r2, bdh, bdu, p_out, c_out):
    r = r2[...]

    for n in range(JK // 2 + 1):
        width = 2 if n < JK // 2 else 1
        part = dot_nt(r, bdh[2 * n * NO : (2 * n + width) * NO, :])
        for half in range(width):
            p_out[(2 * n + half) * 320 : (2 * n + half + 1) * 320, :] = part[
                :, half * NO : (half + 1) * NO
            ]
    for n in range(OT):
        for m in range(5):
            part = dot_nt(
                g2[m * 160 : (m + 1) * 160, :], bdu[2 * n * NO : (2 * n + 2) * NO, :]
            )
            for half in range(2):
                at = (2 * n + half) * 800 + m * 160
                c_out[at : at + 160, :] = part[:, half * NO : (half + 1) * NO]


def weigh(oe_ref, se_ref, base, s, a_in, p_in, c_in, yr, yc):
    start = base + se_ref[s]

    def one(i, _):
        for j in range(OT):
            for k in range(OT):
                jk = j * OT + k
                ki = k * OT + i
                ij = i * OT + j
                energy = (oe_ref[i] + oe_ref[j]) + oe_ref[k]
                tiles = []
                for v in range(4):
                    first = v * 8 * OT * AROWS + s * JK
                    w = a_in[pl.ds(first + i * AROWS + jk, 8, stride=OT * AROWS), :]
                    w = w + a_in[pl.ds(first + j * AROWS + ki, 8, stride=OT * AROWS), :]
                    at = pl.multiple_of(jk * 320 + (s * OT + i) * 32 + v * 8, 8)
                    w = w + p_in[pl.ds(at, 8), :]
                    at = pl.multiple_of(ij * 320 + (s * OT + k) * 32 + v * 8, 8)
                    w = w + p_in[pl.ds(at, 8), :]
                    at = pl.multiple_of((s * OT + j) * 800 + ki * 32 + v * 8, 8)
                    w = w + c_in[pl.ds(at, 8), :]
                    at = pl.multiple_of((s * OT + k) * 800 + ij * 32 + v * 8, 8)
                    w = w + c_in[pl.ds(at, 8), :]
                    tiles.append(w / (start[v * 8 : v * 8 + 8] - energy))
                y = jnp.concatenate(tiles, 0).astype(BF16)
                at = pl.multiple_of((s * OT + i) * 32, 32)
                yr[pl.ds(at, 32), jk * NO : (jk + 1) * NO] = y
                at = pl.multiple_of((s * OT + j) * 800 + ki * 32, 32)
                yc[pl.ds(at, 32), :] = y
        return 0

    lax.fori_loop(0, OT, one, 0)


def deal(res, wide, out):
    for i in range(OT):
        for v in range(OWN):
            wide[pl.ds(v * OT + i, GROUP, stride=PART), :] = res[
                pl.ds(i * 64 + v, GROUP, stride=OWN), :
            ]
    for n in range(GROUP):
        out[n] = wide[n * PART : n * PART + USED, :]


def row_residual(s, bdh, yr, res, wide, row_out):
    out = jnp.dot(yr[s * 160 : (s + 1) * 160, :], bdh[...], preferred_element_type=F32)
    for i in range(OT):
        for half in range(2):
            res[i * 64 + half * 32 : i * 64 + half * 32 + 32, :] = out[
                i * 32 : i * 32 + 32, half * NO : (half + 1) * NO
            ]
    deal(res, wide, row_out)


def col_residual(s, turned, yc, res, wide, col_out):
    lane = lax.broadcasted_iota(jnp.int32, (NO, NO), 1)
    moved = jnp.concatenate(
        [yc[(s * OT + j) * 800 : (s * OT + j + 1) * 800, :] for j in range(OT)], 1
    )
    out = jnp.dot(turned[...], moved, preferred_element_type=F32)
    for j in range(OT):
        piece = out[:, j * NO : (j + 1) * NO]
        both = jnp.where(lane < 64, piece[0:NO], piece[NO:]).T
        res[j * 64 : j * 64 + 64, :] = both[0:64] + both[64:128]
    deal(res, wide, col_out)


class Gather:
    def __init__(self, here, rows, cols, send_sems, row_sems, col_sems):
        self.here, self.rows, self.cols = here, rows, cols
        self.send_sems, self.row_sems, self.col_sems = send_sems, row_sems, col_sems
        self.sent = []

    def copy(self, src, dst, recv_sem, target):
        copy = pltpu.make_async_remote_copy(
            src_ref=src,
            dst_ref=dst,
            send_sem=self.send_sems.at[len(self.sent)],
            recv_sem=recv_sem,
            device_id=target,
            device_id_type=MESH,
        )
        copy.start()
        self.sent.append(copy)

    def row_slot(self, q, k):
        at = (q * 8 + k) * CHUNK
        return self.rows.at[at : at + CHUNK, :]

    def col_slot(self, q, d, c):
        at = pl.multiple_of(self.here.index_a(q, d, c) * CHUNK, 16)
        return self.cols.at[pl.ds(at, CHUNK), :]

    def along_z(self, k):
        self.copy(
            self.row_slot(0, 0), self.row_slot(0, k), self.row_sems.at[0, k],
            self.here.along_b(0, -k),
        )

    def across_x(self, k):
        self.copy(
            self.row_slot(0, k), self.row_slot(1, k), self.row_sems.at[1, k],
            self.here.along_b(1, 0),
        )

    def got_row(self, q, k):
        pltpu.make_async_remote_copy(
            src_ref=self.row_slot(q, k), dst_ref=self.row_slot(q, k),
            send_sem=self.row_sems.at[q, k], recv_sem=self.row_sems.at[q, k],
            device_id=self.here.along_b(0, 1), device_id_type=MESH,
        ).wait_recv()

    def col_to(self, q, d, c, kind, step, target):
        slot = self.col_slot(q, d, c)
        self.copy(slot, slot, self.col_sems.at[kind, step], target)

    def swap_col(self):
        self.col_to(0, 0, 0, 1, 0, self.here.along_a(1, 0, 0))

    def round_col(self, q):
        for d in range(1, 4):
            self.col_to(q, 0, 0, q, d, self.here.along_a(0, -d, 0))

    def twin_col(self, q, d):
        self.col_to(q, d, 0, 2 + q, d, self.here.along_a(0, 0, 1))

    def got_col(self, kind, d):
        slot = self.col_slot(kind % 2, d, kind // 2)
        pltpu.make_async_remote_copy(
            src_ref=slot, dst_ref=slot,
            send_sem=self.col_sems.at[kind, d], recv_sem=self.col_sems.at[kind, d],
            device_id=self.here.along_b(0, 1), device_id_type=MESH,
        ).wait_recv()


def scatter(here, s, along_rows, part, into, send_sems, recv_sems):
    copies = []
    for n in range(1, GROUP):
        if along_rows:
            target = here.along_b(n // 8, n % 8)
            at = n
        else:
            target = here.along_a(n // 8, n // 2 % 4, n % 2)
            at = target[0]
        copy = pltpu.make_async_remote_copy(
            src_ref=part.at[s, at],
            dst_ref=into.at[s, n],
            send_sem=send_sems.at[s, n],
            recv_sem=recv_sems.at[s, n],
            device_id=target,
            device_id_type=MESH,
        )
        copy.start()
        copies.append(copy)
    return copies


def whole_body(
    t_hbm, g_hbm, h_hbm, q_hbm, r_hbm, u_hbm, ve_hbm, oe_hbm, se_hbm,
    row_out, col_out,
    t_ref, g_in, h_in, q_in, r_in, u_in, ve_ref, oe_ref, se_ref,
    q_ref, amp, rows, cols, a_ref, g2, r2, bdh, bdu, p_ref, c_ref, yr, yc, turned, res, wide,
    row_part, col_part, row_into, col_into, last,
    in_sems, gather_sems, row_sems, col_sems, out_row_sems, out_col_sems, sum_row_sems,
    sum_col_sems,
):
    here = Place()
    loads = [
        pltpu.make_async_copy(src, dst, in_sems.at[n])
        for n, (src, dst) in enumerate(
            (
                (g_hbm, g_in), (h_hbm, h_in), (r_hbm, r_in), (u_hbm, u_in), (q_hbm, q_in),
                (ve_hbm, ve_ref), (oe_hbm, oe_ref), (se_hbm, se_ref), (t_hbm, t_ref),
            )
        )
    ]
    for load in loads:
        load.start()
    barrier = pltpu.get_barrier_semaphore()
    near = [here.along_b(0, k) for k in range(1, 8)] + [here.along_b(1, 0)]
    near += [here.along_a(0, d, 0) for d in range(1, 4)]
    near += [here.along_a(1, 0, 0), here.along_a(0, 0, 1)]
    for target in near:
        pl.semaphore_signal(barrier, inc=1, device_id=target, device_id_type=MESH)
    for load in loads[:4]:
        load.wait()
    own_col = cols.at[pl.ds(pl.multiple_of(here.a * CHUNK, 16), CHUNK), :]
    split_l(g_in, h_in, r_in, u_in, rows.at[0:CHUNK, :], own_col, amp)
    pl.semaphore_wait(barrier, len(near))
    net = Gather(here, rows, cols, gather_sems, row_sems, col_sems)
    net.across_x(0)
    for k in ORDER:
        net.along_z(k)
    net.swap_col()
    net.round_col(0)
    net.twin_col(0, 0)
    for load in loads[4:]:
        load.wait()
    split_q(q_in, q_ref)
    net.got_col(1, 0)
    net.round_col(1)
    net.twin_col(1, 0)
    compute_a(here, t_ref, q_ref, a_ref, 0, 4)
    for k in ORDER[0:2]:
        net.got_row(0, k)
        net.across_x(k)
    for d in range(1, 4):
        net.got_col(0, d)
        net.twin_col(0, d)
    compute_a(here, t_ref, q_ref, a_ref, 4, 4)
    for k in ORDER[2:4]:
        net.got_row(0, k)
        net.across_x(k)
    for d in range(1, 4):
        net.got_col(1, d)
        net.twin_col(1, d)
    compute_a(here, t_ref, q_ref, a_ref, 8, 4)
    for k in ORDER[4:6]:
        net.got_row(0, k)
        net.across_x(k)
    compute_a(here, t_ref, q_ref, a_ref, 12, 4)
    for k in ORDER[6:]:
        net.got_row(0, k)
        net.across_x(k)
    clear_off(bdh, bdu)
    for kind in (2, 3):
        for d in range(4):
            net.got_col(kind, d)
    spread(cols, functools.partial(put_cols, bdh, bdu))
    base = pair_energy(here, ve_ref)
    for k in range(8):
        net.got_row(1, k)
    spread(rows, functools.partial(put_rows, g2, r2))
    for copy in net.sent:
        copy.wait_send()
    compute_pc(g2, r2, bdh, bdu, p_ref, c_ref)
    turned[...] = g2[...].T
    sums = [[], []]
    for s in range(NC):
        weigh(oe_ref, se_ref, base, s, a_ref, p_ref, c_ref, yr, yc)
        row_residual(s, bdh, yr, res, wide, row_part.at[s])
        sums[0] += scatter(here, s, True, row_part, row_into, out_row_sems, sum_row_sems)
    for s in range(NC):
        col_residual(s, turned, yc, res, wide, col_part.at[s])
        sums[1] += scatter(here, s, False, col_part, col_into, out_col_sems, sum_col_sems)
    for which, (part, into, out, own) in enumerate(
        (
            (col_part, col_into, col_out, here.a),
            (row_part, row_into, row_out, 0),
        )
    ):
        for s in range(NC):
            total = part[s, own]
            for n in range(1, GROUP):
                sums[1 - which][s * (GROUP - 1) + n - 1].wait_recv()
                total = total + into[s, n]
            last[pl.ds(s, USED, stride=NC), :] = total
        out[...] = last[...]
    for copy in sums[0] + sums[1]:
        copy.wait_send()


def on_device(
    pair_amplitude,
    row_amplitude,
    column_amplitude,
    row_integral,
    column_integral,
    step_integral,
    virtual_energy,
    occupied_energy,
    step_energy,
):
    factor = 1.0 / (math.sqrt(virtual_energy.shape[0]) * OT)
    t = pair_amplitude.transpose(0, 2, 1, 3)
    r = row_amplitude.transpose(0, 2, 1, 3).reshape(OWN * SI, NO)
    u = column_amplitude.transpose(0, 2, 1, 3).reshape(OWN * SI, NO)
    ve = virtual_energy.reshape(8, NO)
    operands = (
        t, row_integral, column_integral, step_integral, r, u, ve, occupied_energy, step_energy
    )
    out = pltpu.VMEM((NC * USED, NO), F32)
    vm = pl.BlockSpec(memory_space=pltpu.VMEM)
    spaces = [pltpu.VMEM] * 7 + [pltpu.SMEM] * 2
    order = range(9)
    dma = pltpu.SemaphoreType.DMA
    results = pl.pallas_call(
        whole_body,
        out_shape=(out, out),
        in_specs=[pl.BlockSpec(memory_space=pl.ANY)] * 9,
        out_specs=(vm, vm),
        scratch_shapes=[spaces[n](operands[n].shape, operands[n].dtype) for n in order]
        + [
            pltpu.VMEM((64, NO), BF16),
            pltpu.VMEM((2, OWN * SI, NO), F32),
            pltpu.VMEM((GROUP * CHUNK, NO), BF16),
            pltpu.VMEM((GROUP * CHUNK, NO), BF16),
            pltpu.VMEM((32 * OT * AROWS, NO), F32),
            pltpu.VMEM((JK * 32, 2 * NO), BF16),
            pltpu.VMEM((SI * 32, 2 * NO), BF16),
            pltpu.VMEM((JK * NO, 2 * NO), BF16),
            pltpu.VMEM((SI * NO, 2 * NO), BF16),
            pltpu.VMEM((JK * 320, NO), F32),
            pltpu.VMEM((SI * 800, NO), F32),
            pltpu.VMEM((320, JK * NO), BF16),
            pltpu.VMEM((SI * 800, NO), BF16),
            pltpu.VMEM((2 * NO, 800), BF16),
            pltpu.VMEM((OT * 64, NO), F32),
            pltpu.VMEM((GROUP * PART, NO), F32),
            pltpu.VMEM((NC, GROUP, USED, NO), F32),
            pltpu.VMEM((NC, GROUP, USED, NO), F32),
            pltpu.VMEM((NC, GROUP, USED, NO), F32),
            pltpu.VMEM((NC, GROUP, USED, NO), F32),
            pltpu.VMEM((NC * USED, NO), F32),
            dma((9,)),
            dma((30,)),
            dma((2, 8)),
            dma((4, 4)),
            dma((NC, GROUP)),
            dma((NC, GROUP)),
            dma((NC, GROUP)),
            dma((NC, GROUP)),
        ],
        compiler_params=pltpu.CompilerParams(
            collective_id=0, has_side_effects=True, vmem_limit_bytes=56 * 2**20
        ),
    )(*operands)
    return tuple(
        (x * factor).reshape(OWN, OT, NC, NO).transpose(0, 2, 1, 3) for x in results
    )


def solution(mesh):
    placed = (
        P("aa", "ba", None, None),
        P(("aa", "ba"), None, None, None),
        P(("ba", "aa"), None, None, None),
        P(("aa", "ba"), None),
        P(("ba", "aa"), None),
        P(),
        P(),
        P(),
        P(),
    )
    return jax.shard_map(
        on_device,
        mesh=mesh,
        in_specs=placed,
        out_specs=(P(("aa", "ba"), None, None, None), P(("ba", "aa"), None, None, None)),
        check_vma=False,
    )
```

```python
import functools
import math

import jax
import jax.numpy as jnp
from jax import lax
from jax.experimental import pallas as pl
from jax.experimental.pallas import tpu as pltpu
from jax.sharding import PartitionSpec as P

F32 = jnp.float32
BF16 = jnp.bfloat16
MESH = pl.DeviceIdType.MESH
GROUP = 16
OWN = 4
OT = 5
JK = OT * OT
NC = 2
SI = OT * NC
NO = 128
CHUNK = 144
PART = 24
USED = OWN * OT
ORDER = (0, 1, 7, 2, 6, 3, 5, 4)
HALF = 4
AROWS = 56
NT = (((1,), (1,)), ((), ()))


def dot_nt(x, y):
    return lax.dot_general(x, y, NT, preferred_element_type=F32)


def by_jk(moved, first, stride, count):
    lane = lax.broadcasted_iota(jnp.int32, (8, NO), 1)
    found = []
    for jk in range(JK):
        source = (JK * ((lane - 41 * jk) & 127) + jk) >> 7
        t = moved[first : first + 8]
        for m in range(1, JK):
            at = first + stride * m
            t = jnp.where(source == m, moved[at : at + 8], t)
        shift = (-41 * jk) % 128
        found.append(pltpu.roll(t, shift, 1) if shift else t)
    return found


def permute_lanes(parts):
    row = lax.broadcasted_iota(jnp.int32, (NO, NO), 0)
    col = lax.broadcasted_iota(jnp.int32, (NO, NO), 1)
    perm = (row == ((JK * col) & 127)).astype(F32).astype(BF16)
    stacked = jnp.concatenate(
        [part[:, m * NO : (m + 1) * NO] for m in range(JK) for part in parts], 0
    ).astype(BF16)
    return jnp.dot(stacked, perm, preferred_element_type=F32)


def put_chunk(tables, src, amp, dst):
    amp[...] = src[...].astype(F32)
    pieces = tables + [
        amp[pl.ds(i * NC + s, OWN, stride=SI), :] for s in range(NC) for i in range(OT)
    ]
    pieces.append(jnp.zeros((4, NO), F32))
    for k in range(9):
        dst[16 * k : 16 * k + 16, :] = jnp.concatenate(
            pieces[4 * k : 4 * k + 4], 0
        ).astype(BF16)


def split_q(q_ref, q_out):
    low = jnp.concatenate([q_ref[...].astype(F32), jnp.zeros((6, JK * NO), F32)], 0)
    lows = by_jk(permute_lanes([low]), 0, 8, JK)
    rows = [lows[jk][s : s + 1] for s in range(NC) for jk in range(JK)]
    rows.append(jnp.zeros((64 - NC * JK, NO), F32))
    q_out[...] = jnp.concatenate(rows, 0).astype(BF16)


def split_l(g_ref, h_ref, r_ref, u_ref, row_chunk, col_chunk, amp):
    top = jnp.concatenate([g_ref[...].astype(F32), h_ref[...].astype(F32)], 0)
    tops = by_jk(permute_lanes([top]), 0, 8, JK)
    put_chunk([t[0:4] for t in tops], r_ref, amp.at[0], row_chunk)
    put_chunk([t[4:8] for t in tops], u_ref, amp.at[1], col_chunk)


class Place:
    def __init__(self):
        self.a = lax.axis_index("aa")
        self.b = lax.axis_index("ba")
        self.core = lax.rem(self.a, 2)
        self.y = lax.rem(self.a // 2, 4)
        self.xl = self.a // 8
        self.xh = self.b // 8
        self.z = lax.rem(self.b, 8)

    def index_b(self, q, k):
        xh = 1 - self.xh if q else self.xh
        return xh * 8 + lax.rem(self.z - k + 8, 8)

    def along_b(self, q, k):
        return (self.a, self.index_b(q, k))

    def index_a(self, q, d, c):
        xl = 1 - self.xl if q else self.xl
        core = 1 - self.core if c else self.core
        return (xl * 4 + lax.rem(self.y - d + 4, 4)) * 2 + core

    def along_a(self, q, d, c):
        return (self.index_a(q, d, c), self.b)


def compute_a(here, t_ref, q_ref, a_out, first, count):
    q = q_ref[0:AROWS, :]
    for at_k in range(first, first + count):
        zk = lax.rem(here.z - ORDER[at_k] + 8, 8)
        near_k = (here.xh * 8 + zk) * OWN
        far_k = ((1 - here.xh) * 8 + zk) * OWN

        def pair(n, _, at_k=at_k, near_k=near_k, far_k=far_k):
            near, far = near_k + 2 * n, far_k + 2 * n
            for i in range(OT):
                block = jnp.concatenate(
                    [t_ref[near, i], t_ref[far, i], t_ref[near + 1, i], t_ref[far + 1, i]],
                    0,
                )
                part = dot_nt(q, block)
                for half in range(2):
                    at = pl.multiple_of(
                        (4 * at_k + 2 * n + half) * (OT * AROWS) + i * AROWS, 8
                    )
                    a_out[pl.ds(at, AROWS), :] = part[:, half * NO : (half + 1) * NO]
            return 0

        lax.fori_loop(0, 2, pair, 0)


def pair_energy(here, ve_ref):
    lane = lax.broadcasted_iota(jnp.int32, (32, NO), 1)
    row = lax.broadcasted_iota(jnp.int32, (32, NO), 0)
    offset = jnp.zeros((32, NO), jnp.int32)
    for at_k, k in enumerate(ORDER):
        offset = jnp.where((row >> 2) == at_k, k, offset)
    zk = (here.z - offset) & 7
    lead = jnp.broadcast_to(ve_ref[pl.ds(here.a // 2, 1), :], (32, NO))
    first = lax.rem(here.a, 2) * 64
    halves = []
    for xh in (here.xh, 1 - here.xh):
        at = first + (xh * 8 + zk) * OWN + (row & 3)
        halves.append(jnp.sum(jnp.where(lane == at, lead, 0.0), 1, keepdims=True))
    tail = ve_ref[pl.ds(here.b // 2, 1), :]
    turned = pltpu.roll(jnp.broadcast_to(tail, (8, NO)), 64, 1)[0:1]
    keep = (lane[0:1] // 64) == lax.rem(here.b, 2)
    tail = jnp.where(keep, tail, turned)
    return jnp.where(lane < 64, halves[0], halves[1]) + tail


def spread(src, wide):
    for k in range(9):
        blocks = [
            src[e * CHUNK + 16 * k : e * CHUNK + 16 * k + 16, :].astype(F32)
            for e in range(GROUP)
        ]
        for c in range(4):
            at = 4 * k + c
            if at >= JK + SI:
                continue
            tile = jnp.concatenate([b[4 * c : 4 * c + 4] for b in blocks], 0)
            wide(at, tile.astype(BF16))


def spread_rows(group, rows, g2, r2):
    for k in range(9):
        for q in range(2):
            blocks = []
            for offset in ORDER[group * HALF : (group + 1) * HALF]:
                at = (q * 8 + offset) * CHUNK + 16 * k
                blocks.append(rows[at : at + 16, :].astype(F32))
            for c in range(4):
                at = 4 * k + c
                if at >= JK + SI:
                    continue
                tile = jnp.concatenate([b[4 * c : 4 * c + 4] for b in blocks], 0)
                dst, to = (g2, at) if at < JK else (r2, at - JK)
                dst[to * 16 : to * 16 + 16, q * NO : (q + 1) * NO] = tile.astype(BF16)


def put_cols(bdh, bdu, at, tile):
    dst, c = (bdh, at) if at < JK else (bdu, at - JK)
    dst[c * NO : c * NO + 64, 0:NO] = tile
    dst[c * NO + 64 : c * NO + NO, NO : 2 * NO] = tile


def clear_off(bdh, bdu):
    zero = jnp.zeros((64, NO), BF16)
    for dst, count in ((bdh, JK), (bdu, SI)):
        for c in range(count):
            dst[c * NO : c * NO + 64, NO : 2 * NO] = zero
            dst[c * NO + 64 : c * NO + NO, 0:NO] = zero


def compute_pc(g2, r2, bdh, bdu, p_out, c_out):
    r = r2[...]
    for n in range(JK // 2 + 1):
        width = 2 if n < JK // 2 else 1
        part = dot_nt(r, bdh[2 * n * NO : (2 * n + width) * NO, :])
        for half in range(width):
            p_out[(2 * n + half) * 160 : (2 * n + half + 1) * 160, :] = part[
                :, half * NO : (half + 1) * NO
            ]
    for n in range(OT):
        part = dot_nt(g2[...], bdu[2 * n * NO : (2 * n + 2) * NO, :])
        for half in range(2):
            at = (2 * n + half) * 400
            c_out[at : at + 400, :] = part[:, half * NO : (half + 1) * NO]


def weigh(oe_ref, se_ref, base, group, s, a_in, p_in, c_in, yr, yc):
    start = base + se_ref[s]

    def one(i, _):
        for j in range(OT):
            for k in range(OT):
                jk = j * OT + k
                ki = k * OT + i
                ij = i * OT + j
                energy = (oe_ref[i] + oe_ref[j]) + oe_ref[k]
                tiles = []
                for v in range(2):
                    row = group * 16 + v * 8
                    first = row * OT * AROWS + s * JK
                    w = a_in[pl.ds(first + i * AROWS + jk, 8, stride=OT * AROWS), :]
                    w = w + a_in[pl.ds(first + j * AROWS + ki, 8, stride=OT * AROWS), :]
                    at = pl.multiple_of(jk * 160 + (s * OT + i) * 16 + v * 8, 8)
                    w = w + p_in[pl.ds(at, 8), :]
                    at = pl.multiple_of(ij * 160 + (s * OT + k) * 16 + v * 8, 8)
                    w = w + p_in[pl.ds(at, 8), :]
                    at = pl.multiple_of((s * OT + j) * 400 + ki * 16 + v * 8, 8)
                    w = w + c_in[pl.ds(at, 8), :]
                    at = pl.multiple_of((s * OT + k) * 400 + ij * 16 + v * 8, 8)
                    w = w + c_in[pl.ds(at, 8), :]
                    tiles.append(w / (start[row : row + 8] - energy))
                y = jnp.concatenate(tiles, 0).astype(BF16)
                at = pl.multiple_of((s * OT + i) * 16, 16)
                yr[pl.ds(at, 16), jk * NO : (jk + 1) * NO] = y
                at = pl.multiple_of((s * OT + j) * 400 + ki * 16, 16)
                yc[pl.ds(at, 16), :] = y
        return 0

    lax.fori_loop(0, OT, one, 0)


def deal(res, wide, out):
    for i in range(OT):
        for v in range(OWN):
            wide[pl.ds(v * OT + i, GROUP, stride=PART), :] = res[
                pl.ds(i * 64 + v, GROUP, stride=OWN), :
            ]
    for n in range(GROUP):
        out[n] = wide[n * PART : n * PART + USED, :]


def row_residual(bdh, yr, res, row_out):
    out = jnp.dot(yr[...], bdh[...], preferred_element_type=F32)
    for c in range(SI):
        for q in range(2):
            res[c * 32 + q * 16 : c * 32 + q * 16 + 16, :] = out[
                c * 16 : c * 16 + 16, q * NO : (q + 1) * NO
            ]
    for c in range(SI):
        for v in range(OWN):
            at = v * SI + c % OT * NC + c // OT
            row_out[pl.ds(at, 2 * HALF, stride=OWN * SI), :] = res[
                pl.ds(c * 32 + v, 2 * HALF, stride=OWN), :
            ]


def col_products(s, turned, yc):
    lane = lax.broadcasted_iota(jnp.int32, (NO, NO), 1)
    moved = jnp.concatenate(
        [yc[(s * OT + j) * 400 : (s * OT + j + 1) * 400, :] for j in range(OT)], 1
    )
    out = jnp.dot(turned, moved, preferred_element_type=F32)
    pieces = [out[:, j * NO : (j + 1) * NO] for j in range(OT)]
    return [jnp.where(lane < 64, piece[0:NO], piece[NO:]) for piece in pieces]


def col_first(s, turned, yc, held):
    for j, piece in enumerate(col_products(s, turned, yc)):
        held[s * OT + j] = piece


def col_residual(s, turned, yc, held, res, wide, col_out):
    for j, piece in enumerate(col_products(s, turned, yc)):
        both = (piece + held[s * OT + j]).T
        res[j * 64 : j * 64 + 64, :] = both[0:64] + both[64:128]
    deal(res, wide, col_out)


class Gather:
    def __init__(self, here, rows, cols, send_sems, row_sems, col_sems):
        self.here, self.rows, self.cols = here, rows, cols
        self.send_sems, self.row_sems, self.col_sems = send_sems, row_sems, col_sems
        self.sent = []

    def copy(self, src, dst, recv_sem, target):
        copy = pltpu.make_async_remote_copy(
            src_ref=src,
            dst_ref=dst,
            send_sem=self.send_sems.at[len(self.sent)],
            recv_sem=recv_sem,
            device_id=target,
            device_id_type=MESH,
        )
        copy.start()
        self.sent.append(copy)

    def row_slot(self, q, k):
        at = (q * 8 + k) * CHUNK
        return self.rows.at[at : at + CHUNK, :]

    def col_slot(self, q, d, c):
        at = pl.multiple_of(self.here.index_a(q, d, c) * CHUNK, 16)
        return self.cols.at[pl.ds(at, CHUNK), :]

    def along_z(self, k):
        self.copy(
            self.row_slot(0, 0), self.row_slot(0, k), self.row_sems.at[0, k],
            self.here.along_b(0, -k),
        )

    def across_x(self, k):
        self.copy(
            self.row_slot(0, k), self.row_slot(1, k), self.row_sems.at[1, k],
            self.here.along_b(1, 0),
        )

    def got_row(self, q, k):
        pltpu.make_async_remote_copy(
            src_ref=self.row_slot(q, k), dst_ref=self.row_slot(q, k),
            send_sem=self.row_sems.at[q, k], recv_sem=self.row_sems.at[q, k],
            device_id=self.here.along_b(0, 1), device_id_type=MESH,
        ).wait_recv()

    def col_to(self, q, d, c, kind, step, target):
        slot = self.col_slot(q, d, c)
        self.copy(slot, slot, self.col_sems.at[kind, step], target)

    def swap_col(self):
        self.col_to(0, 0, 0, 1, 0, self.here.along_a(1, 0, 0))

    def round_col(self, q):
        for d in range(1, 4):
            self.col_to(q, 0, 0, q, d, self.here.along_a(0, -d, 0))

    def twin_col(self, q, d):
        self.col_to(q, d, 0, 2 + q, d, self.here.along_a(0, 0, 1))

    def got_col(self, kind, d):
        slot = self.col_slot(kind % 2, d, kind // 2)
        pltpu.make_async_remote_copy(
            src_ref=slot, dst_ref=slot,
            send_sem=self.col_sems.at[kind, d], recv_sem=self.col_sems.at[kind, d],
            device_id=self.here.along_b(0, 1), device_id_type=MESH,
        ).wait_recv()


def send_part(src, dst, send_sem, recv_sem, target):
    copy = pltpu.make_async_remote_copy(
        src_ref=src,
        dst_ref=dst,
        send_sem=send_sem,
        recv_sem=recv_sem,
        device_id=target,
        device_id_type=MESH,
    )
    copy.start()
    return copy


def scatter_rows(here, group, part, into, send_sems, recv_sems):
    copies = []
    for q in (1, 0):
        for p in reversed(range(HALF)):
            k = ORDER[group * HALF + p]
            if q == 0 and k == 0:
                continue
            at = (q * HALF + p) * OWN * SI
            copies.append(
                send_part(
                    part.at[group, at : at + OWN * SI, :], into.at[q * 8 + k],
                    send_sems.at[q * 8 + k], recv_sems.at[q * 8 + k], here.along_b(q, k),
                )
            )
    return copies


def scatter_cols(here, s, part, into, send_sems, recv_sems):
    copies = []
    for n in range(1, GROUP):
        target = here.along_a(n // 8, n // 2 % 4, n % 2)
        copies.append(
            send_part(
                part.at[s, target[0]], into.at[s, n], send_sems.at[s, n],
                recv_sems.at[s, n], target,
            )
        )
    return copies


def whole_body(
    t_hbm, g_hbm, h_hbm, q_hbm, r_hbm, u_hbm, ve_hbm, oe_hbm, se_hbm,
    row_out, col_out,
    t_ref, g_in, h_in, q_in, r_in, u_in, ve_ref, oe_ref, se_ref,
    q_ref, amp, rows, cols, a_ref, g2, r2, bdh, bdu, p_ref, c_ref, yr, yc, res, wide, held,
    row_part, col_part, row_into, col_into, last,
    in_sems, gather_sems, row_sems, col_sems, out_row_sems, out_col_sems, sum_row_sems,
    sum_col_sems,
):
    here = Place()
    loads = [
        pltpu.make_async_copy(src, dst, in_sems.at[n])
        for n, (src, dst) in enumerate(
            (
                (g_hbm, g_in), (h_hbm, h_in), (r_hbm, r_in), (u_hbm, u_in), (q_hbm, q_in),
                (ve_hbm, ve_ref), (oe_hbm, oe_ref), (se_hbm, se_ref), (t_hbm, t_ref),
            )
        )
    ]
    for load in loads:
        load.start()
    barrier = pltpu.get_barrier_semaphore()
    near = [here.along_b(0, k) for k in range(1, 8)] + [here.along_b(1, 0)]
    near += [here.along_a(0, d, 0) for d in range(1, 4)]
    near += [here.along_a(1, 0, 0), here.along_a(0, 0, 1)]
    for target in near:
        pl.semaphore_signal(barrier, inc=1, device_id=target, device_id_type=MESH)
    for load in loads[:4]:
        load.wait()
    own_col = cols.at[pl.ds(pl.multiple_of(here.a * CHUNK, 16), CHUNK), :]
    split_l(g_in, h_in, r_in, u_in, rows.at[0:CHUNK, :], own_col, amp)
    pl.semaphore_wait(barrier, len(near))
    net = Gather(here, rows, cols, gather_sems, row_sems, col_sems)
    net.across_x(0)
    for k in ORDER:
        if k:
            net.along_z(k)
    net.swap_col()
    net.round_col(0)
    net.twin_col(0, 0)
    for load in loads[4:]:
        load.wait()
    split_q(q_in, q_ref)
    net.got_col(1, 0)
    net.round_col(1)
    net.twin_col(1, 0)
    compute_a(here, t_ref, q_ref, a_ref, 0, 2)
    others = [k for k in ORDER if k]
    for k in others[0:2]:
        net.got_row(0, k)
        net.across_x(k)
    for d in range(1, 4):
        net.got_col(0, d)
        net.twin_col(0, d)
    compute_a(here, t_ref, q_ref, a_ref, 2, 2)
    for k in others[2:4]:
        net.got_row(0, k)
        net.across_x(k)
    for d in range(1, 4):
        net.got_col(1, d)
        net.twin_col(1, d)
    compute_a(here, t_ref, q_ref, a_ref, 4, 2)
    for k in others[4:6]:
        net.got_row(0, k)
        net.across_x(k)
    compute_a(here, t_ref, q_ref, a_ref, 6, 2)
    for k in others[6:]:
        net.got_row(0, k)
        net.across_x(k)
    clear_off(bdh, bdu)
    for kind in (2, 3):
        for d in range(4):
            net.got_col(kind, d)
    spread(cols, functools.partial(put_cols, bdh, bdu))
    base = pair_energy(here, ve_ref)
    row_sums, col_sums = [], []
    for group in range(2):
        for k in ORDER[group * HALF : (group + 1) * HALF]:
            net.got_row(1, k)
        spread_rows(group, rows, g2, r2)
        compute_pc(g2, r2, bdh, bdu, p_ref, c_ref)
        for s in range(NC):
            weigh(oe_ref, se_ref, base, group, s, a_ref, p_ref, c_ref, yr, yc)
        row_residual(bdh, yr, res, row_part.at[group])
        row_sums += scatter_rows(
            here, group, row_part, row_into, out_row_sems, sum_row_sems
        )
        turned = g2[...].T
        for s in range(NC):
            if group == 0:
                col_first(s, turned, yc, held)
                continue
            col_residual(s, turned, yc, held, res, wide, col_part.at[s])
            col_sums += scatter_cols(
                here, s, col_part, col_into, out_col_sems, sum_col_sems
            )
    for copy in net.sent:
        copy.wait_send()
    for s in range(NC):
        total = col_part[s, here.a]
        for n in range(1, GROUP):
            col_sums[s * (GROUP - 1) + n - 1].wait_recv()
            total = total + col_into[s, n]
        last[pl.ds(s, USED, stride=NC), :] = total
    col_out[...] = last[...]
    at = ORDER.index(0)
    total = row_part[at // HALF, at % HALF * OWN * SI : (at % HALF + 1) * OWN * SI, :]
    for copy in row_sums:
        copy.wait_recv()
    for n in range(1, GROUP):
        total = total + row_into[n]
    row_out[...] = total
    for copy in row_sums + col_sums:
        copy.wait_send()


def on_device(
    pair_amplitude,
    row_amplitude,
    column_amplitude,
    row_integral,
    column_integral,
    step_integral,
    virtual_energy,
    occupied_energy,
    step_energy,
):
    factor = 1.0 / (math.sqrt(virtual_energy.shape[0]) * OT)
    t = pair_amplitude.transpose(0, 2, 1, 3)
    r = row_amplitude.transpose(0, 2, 1, 3).reshape(OWN * SI, NO)
    u = column_amplitude.transpose(0, 2, 1, 3).reshape(OWN * SI, NO)
    ve = virtual_energy.reshape(8, NO)
    operands = (
        t, row_integral, column_integral, step_integral, r, u, ve, occupied_energy, step_energy
    )
    out = pltpu.VMEM((NC * USED, NO), F32)
    vm = pl.BlockSpec(memory_space=pltpu.VMEM)
    spaces = [pltpu.VMEM] * 7 + [pltpu.SMEM] * 2
    order = range(9)
    dma = pltpu.SemaphoreType.DMA
    results = pl.pallas_call(
        whole_body,
        out_shape=(out, out),
        in_specs=[pl.BlockSpec(memory_space=pl.ANY)] * 9,
        out_specs=(vm, vm),
        scratch_shapes=[spaces[n](operands[n].shape, operands[n].dtype) for n in order]
        + [
            pltpu.VMEM((64, NO), BF16),
            pltpu.VMEM((2, OWN * SI, NO), F32),
            pltpu.VMEM((GROUP * CHUNK, NO), BF16),
            pltpu.VMEM((GROUP * CHUNK, NO), BF16),
            pltpu.VMEM((32 * OT * AROWS, NO), F32),
            pltpu.VMEM((JK * 16, 2 * NO), BF16),
            pltpu.VMEM((SI * 16, 2 * NO), BF16),
            pltpu.VMEM((JK * NO, 2 * NO), BF16),
            pltpu.VMEM((SI * NO, 2 * NO), BF16),
            pltpu.VMEM((JK * 160, NO), F32),
            pltpu.VMEM((SI * 400, NO), F32),
            pltpu.VMEM((160, JK * NO), BF16),
            pltpu.VMEM((SI * 400, NO), BF16),
            pltpu.VMEM((OT * 64, NO), F32),
            pltpu.VMEM((GROUP * PART, NO), F32),
            pltpu.VMEM((SI, NO, NO), F32),
            pltpu.VMEM((2, 2 * HALF * OWN * SI, NO), F32),
            pltpu.VMEM((NC, GROUP, USED, NO), F32),
            pltpu.VMEM((GROUP, OWN * SI, NO), F32),
            pltpu.VMEM((NC, GROUP, USED, NO), F32),
            pltpu.VMEM((NC * USED, NO), F32),
            dma((9,)),
            dma((30,)),
            dma((2, 8)),
            dma((4, 4)),
            dma((GROUP,)),
            dma((NC, GROUP)),
            dma((GROUP,)),
            dma((NC, GROUP)),
        ],
        compiler_params=pltpu.CompilerParams(
            collective_id=0, has_side_effects=True, vmem_limit_bytes=56 * 2**20
        ),
    )(*operands)
    return tuple(
        (x * factor).reshape(OWN, OT, NC, NO).transpose(0, 2, 1, 3) for x in results
    )


def solution(mesh):
    placed = (
        P("aa", "ba", None, None),
        P(("aa", "ba"), None, None, None),
        P(("ba", "aa"), None, None, None),
        P(("aa", "ba"), None),
        P(("ba", "aa"), None),
        P(),
        P(),
        P(),
        P(),
    )
    return jax.shard_map(
        on_device,
        mesh=mesh,
        in_specs=placed,
        out_specs=(P(("aa", "ba"), None, None, None), P(("ba", "aa"), None, None, None)),
        check_vma=False,
    )
```

```python
import functools
import math

import jax
import jax.numpy as jnp
from jax import lax
from jax.experimental import pallas as pl
from jax.experimental.pallas import tpu as pltpu
from jax.sharding import PartitionSpec as P

F32 = jnp.float32
BF16 = jnp.bfloat16
MESH = pl.DeviceIdType.MESH
GROUP = 16
OWN = 4
OT = 5
JK = OT * OT
NC = 2
SI = OT * NC
NO = 128
CHUNK = 144
USED = OWN * OT
ORDER = (0, 1, 7, 2, 6, 3, 5, 4)
HALF = 4
AROWS = 56
NT = (((1,), (1,)), ((), ()))


def dot_nt(x, y):
    return lax.dot_general(x, y, NT, preferred_element_type=F32)


def by_jk(moved, first, stride, count):
    lane = lax.broadcasted_iota(jnp.int32, (8, NO), 1)
    found = []
    for jk in range(JK):
        source = (JK * ((lane - 41 * jk) & 127) + jk) >> 7
        t = moved[first : first + 8]
        for m in range(1, JK):
            at = first + stride * m
            t = jnp.where(source == m, moved[at : at + 8], t)
        shift = (-41 * jk) % 128
        found.append(pltpu.roll(t, shift, 1) if shift else t)
    return found


def permute_lanes(parts):
    row = lax.broadcasted_iota(jnp.int32, (NO, NO), 0)
    col = lax.broadcasted_iota(jnp.int32, (NO, NO), 1)
    perm = (row == ((JK * col) & 127)).astype(F32).astype(BF16)
    stacked = jnp.concatenate(
        [part[:, m * NO : (m + 1) * NO] for m in range(JK) for part in parts], 0
    ).astype(BF16)
    return jnp.dot(stacked, perm, preferred_element_type=F32)


def put_chunk(tables, src, amp, dst):
    amp[...] = src[...].astype(F32)
    pieces = tables + [
        amp[pl.ds(i * NC + s, OWN, stride=SI), :] for s in range(NC) for i in range(OT)
    ]
    pieces.append(jnp.zeros((4, NO), F32))
    for k in range(9):
        dst[16 * k : 16 * k + 16, :] = jnp.concatenate(
            pieces[4 * k : 4 * k + 4], 0
        ).astype(BF16)


def split_q(q_ref, q_out):
    low = jnp.concatenate([q_ref[...].astype(F32), jnp.zeros((6, JK * NO), F32)], 0)
    lows = by_jk(permute_lanes([low]), 0, 8, JK)
    rows = [lows[jk][s : s + 1] for s in range(NC) for jk in range(JK)]
    rows.append(jnp.zeros((64 - NC * JK, NO), F32))
    q_out[...] = jnp.concatenate(rows, 0).astype(BF16)


def split_l(g_ref, h_ref, r_ref, u_ref, row_chunk, col_chunk, amp):
    top = jnp.concatenate([g_ref[...].astype(F32), h_ref[...].astype(F32)], 0)
    tops = by_jk(permute_lanes([top]), 0, 8, JK)
    put_chunk([t[0:4] for t in tops], r_ref, amp.at[0], row_chunk)
    put_chunk([t[4:8] for t in tops], u_ref, amp.at[1], col_chunk)


class Place:
    def __init__(self):
        self.a = lax.axis_index("aa")
        self.b = lax.axis_index("ba")
        self.core = lax.rem(self.a, 2)
        self.y = lax.rem(self.a // 2, 4)
        self.xl = self.a // 8
        self.xh = self.b // 8
        self.z = lax.rem(self.b, 8)

    def index_b(self, q, k):
        xh = 1 - self.xh if q else self.xh
        return xh * 8 + lax.rem(self.z - k + 8, 8)

    def along_b(self, q, k):
        return (self.a, self.index_b(q, k))

    def index_a(self, q, d, c):
        xl = 1 - self.xl if q else self.xl
        core = 1 - self.core if c else self.core
        return (xl * 4 + lax.rem(self.y - d + 4, 4)) * 2 + core

    def along_a(self, q, d, c):
        return (self.index_a(q, d, c), self.b)


def compute_a(here, t_ref, q_ref, a_out, first, count):
    q = q_ref[0:AROWS, :]
    for at_k in range(first, first + count):
        zk = lax.rem(here.z - ORDER[at_k] + 8, 8)
        near_k = (here.xh * 8 + zk) * OWN
        far_k = ((1 - here.xh) * 8 + zk) * OWN

        def pair(n, _, at_k=at_k, near_k=near_k, far_k=far_k):
            near, far = near_k + 2 * n, far_k + 2 * n
            for i in range(OT):
                block = jnp.concatenate(
                    [t_ref[near, i], t_ref[far, i], t_ref[near + 1, i], t_ref[far + 1, i]],
                    0,
                )
                part = dot_nt(q, block)
                for half in range(2):
                    at = pl.multiple_of(
                        (4 * at_k + 2 * n + half) * (OT * AROWS) + i * AROWS, 8
                    )
                    a_out[pl.ds(at, AROWS), :] = part[:, half * NO : (half + 1) * NO]
            return 0

        lax.fori_loop(0, 2, pair, 0)


def pair_energy(here, ve_ref):
    lane = lax.broadcasted_iota(jnp.int32, (32, NO), 1)
    row = lax.broadcasted_iota(jnp.int32, (32, NO), 0)
    offset = jnp.zeros((32, NO), jnp.int32)
    for at_k, k in enumerate(ORDER):
        offset = jnp.where((row >> 2) == at_k, k, offset)
    zk = (here.z - offset) & 7
    lead = jnp.broadcast_to(ve_ref[pl.ds(here.a // 2, 1), :], (32, NO))
    first = lax.rem(here.a, 2) * 64
    halves = []
    for xh in (here.xh, 1 - here.xh):
        at = first + (xh * 8 + zk) * OWN + (row & 3)
        halves.append(jnp.sum(jnp.where(lane == at, lead, 0.0), 1, keepdims=True))
    tail = ve_ref[pl.ds(here.b // 2, 1), :]
    turned = pltpu.roll(jnp.broadcast_to(tail, (8, NO)), 64, 1)[0:1]
    keep = (lane[0:1] // 64) == lax.rem(here.b, 2)
    tail = jnp.where(keep, tail, turned)
    return jnp.where(lane < 64, halves[0], halves[1]) + tail


def spread(src, wide):
    for k in range(9):
        blocks = [
            src[e * CHUNK + 16 * k : e * CHUNK + 16 * k + 16, :].astype(F32)
            for e in range(GROUP)
        ]
        for c in range(4):
            at = 4 * k + c
            if at >= JK + SI:
                continue
            tile = jnp.concatenate([b[4 * c : 4 * c + 4] for b in blocks], 0)
            wide(at, tile.astype(BF16))


def spread_rows(group, rows, g2, r2):
    for k in range(9):
        for q in range(2):
            blocks = []
            for offset in ORDER[group * HALF : (group + 1) * HALF]:
                at = (q * 8 + offset) * CHUNK + 16 * k
                blocks.append(rows[at : at + 16, :].astype(F32))
            for c in range(4):
                at = 4 * k + c
                if at >= JK + SI:
                    continue
                tile = jnp.concatenate([b[4 * c : 4 * c + 4] for b in blocks], 0)
                dst, to = (g2, at) if at < JK else (r2, at - JK)
                dst[to * 16 : to * 16 + 16, q * NO : (q + 1) * NO] = tile.astype(BF16)


def put_cols(bdh, bdu, at, tile):
    dst, c = (bdh, at) if at < JK else (bdu, at - JK)
    dst[c * NO : c * NO + 64, 0:NO] = tile
    dst[c * NO + 64 : c * NO + NO, NO : 2 * NO] = tile


def clear_off(bdh, bdu):
    zero = jnp.zeros((64, NO), BF16)
    for dst, count in ((bdh, JK), (bdu, SI)):
        for c in range(count):
            dst[c * NO : c * NO + 64, NO : 2 * NO] = zero
            dst[c * NO + 64 : c * NO + NO, 0:NO] = zero


def compute_pc(g2, r2, bdh, bdu, p_out, c_out):
    r = r2[...]
    for n in range(JK // 2 + 1):
        width = 2 if n < JK // 2 else 1
        part = dot_nt(r, bdh[2 * n * NO : (2 * n + width) * NO, :])
        for half in range(width):
            p_out[(2 * n + half) * 160 : (2 * n + half + 1) * 160, :] = part[
                :, half * NO : (half + 1) * NO
            ]
    for n in range(OT):
        part = dot_nt(g2[...], bdu[2 * n * NO : (2 * n + 2) * NO, :])
        for half in range(2):
            at = (2 * n + half) * 400
            c_out[at : at + 400, :] = part[:, half * NO : (half + 1) * NO]


def cycles():
    found, seen = [], set()
    for n in range(OT**3):
        i, j, k = n // JK, n // OT % OT, n % OT
        if (i, j, k) not in seen:
            turns = [(i, j, k), (j, k, i), (k, i, j)]
            found.append(turns if i != j or j != k else turns[:1])
            seen.update(turns)
    return found


def weigh(oe_ref, se_ref, base, group, s, a_in, p_in, c_in, yr, yc):
    start = base[group * 16 : group * 16 + 16] + se_ref[s]
    first = group * 16 * OT * AROWS + s * JK
    for turns in cycles():
        i, j, k = turns[0]
        inverse = 1.0 / (start - ((oe_ref[i] + oe_ref[j]) + oe_ref[k]))
        a, p, c = [], [], []
        for x, y, z in turns:
            yz = y * OT + z
            at = first + x * AROWS + yz
            a.append(a_in[pl.ds(at, 16, stride=OT * AROWS), :])
            at = yz * 160 + (s * OT + x) * 16
            p.append(p_in[at : at + 16, :])
            at = (s * OT + x) * 400 + yz * 16
            c.append(c_in[at : at + 16, :])
        count = len(turns)
        for n, (x, y, z) in enumerate(turns):
            one, two = (n + 1) % count, (n + 2) % count
            w = (a[n] + a[one]) + (p[n] + p[two]) + (c[one] + c[two])
            out = (w * inverse).astype(BF16)
            yz = y * OT + z
            at = (s * OT + x) * 16
            yr[at : at + 16, yz * NO : (yz + 1) * NO] = out
            at = (s * OT + y) * 400 + (z * OT + x) * 16
            yc[at : at + 16, :] = out


def row_residual(bdh, yr, res, row_out):
    out = jnp.dot(yr[...], bdh[...], preferred_element_type=F32)
    for c in range(SI):
        for q in range(2):
            res[c * 32 + q * 16 : c * 32 + q * 16 + 16, :] = out[
                c * 16 : c * 16 + 16, q * NO : (q + 1) * NO
            ]
    for c in range(SI):
        for v in range(OWN):
            at = v * SI + c % OT * NC + c // OT
            row_out[pl.ds(at, 2 * HALF, stride=OWN * SI), :] = res[
                pl.ds(c * 32 + v, 2 * HALF, stride=OWN), :
            ]


def col_products(s, turned, yc):
    lane = lax.broadcasted_iota(jnp.int32, (NO, NO), 1)
    moved = jnp.concatenate(
        [yc[(s * OT + j) * 400 : (s * OT + j + 1) * 400, :] for j in range(OT)], 1
    )
    out = jnp.dot(turned, moved, preferred_element_type=F32)
    pieces = [out[:, j * NO : (j + 1) * NO] for j in range(OT)]
    return [jnp.where(lane < 64, piece[0:NO], piece[NO:]) for piece in pieces]


def col_first(s, turned, yc, held):
    for j, piece in enumerate(col_products(s, turned, yc)):
        held[s * OT + j] = piece


def col_residual(s, turned, yc, held, res, col_out):
    for j, piece in enumerate(col_products(s, turned, yc)):
        both = (piece + held[s * OT + j]).T
        res[j * 64 : j * 64 + 64, :] = both[0:64] + both[64:128]
    for j in range(OT):
        for core in range(2):
            for v in range(OWN):
                col_out[core, pl.ds(v * SI + j * NC + s, 8, stride=OWN * SI), :] = res[
                    pl.ds(j * 64 + core * OWN + v, 8, stride=2 * OWN), :
                ]


class Gather:
    def __init__(self, here, rows, cols, send_sems, row_sems, col_sems):
        self.here, self.rows, self.cols = here, rows, cols
        self.send_sems, self.row_sems, self.col_sems = send_sems, row_sems, col_sems
        self.sent = []

    def copy(self, src, dst, recv_sem, target):
        copy = pltpu.make_async_remote_copy(
            src_ref=src,
            dst_ref=dst,
            send_sem=self.send_sems.at[len(self.sent)],
            recv_sem=recv_sem,
            device_id=target,
            device_id_type=MESH,
        )
        copy.start()
        self.sent.append(copy)

    def row_slot(self, q, k):
        at = (q * 8 + k) * CHUNK
        return self.rows.at[at : at + CHUNK, :]

    def col_slot(self, q, d, c):
        at = pl.multiple_of(self.here.index_a(q, d, c) * CHUNK, 16)
        return self.cols.at[pl.ds(at, CHUNK), :]

    def along_z(self, k):
        self.copy(
            self.row_slot(0, 0), self.row_slot(0, k), self.row_sems.at[0, k],
            self.here.along_b(0, -k),
        )

    def across_x(self, k):
        self.copy(
            self.row_slot(0, k), self.row_slot(1, k), self.row_sems.at[1, k],
            self.here.along_b(1, 0),
        )

    def got_row(self, q, k):
        pltpu.make_async_remote_copy(
            src_ref=self.row_slot(q, k), dst_ref=self.row_slot(q, k),
            send_sem=self.row_sems.at[q, k], recv_sem=self.row_sems.at[q, k],
            device_id=self.here.along_b(0, 1), device_id_type=MESH,
        ).wait_recv()

    def col_to(self, q, d, c, kind, step, target):
        slot = self.col_slot(q, d, c)
        self.copy(slot, slot, self.col_sems.at[kind, step], target)

    def swap_col(self):
        self.col_to(0, 0, 0, 1, 0, self.here.along_a(1, 0, 0))

    def round_col(self, q):
        for d in range(1, 4):
            self.col_to(q, 0, 0, q, d, self.here.along_a(0, -d, 0))

    def twin_col(self, q, d):
        self.col_to(q, d, 0, 2 + q, d, self.here.along_a(0, 0, 1))

    def got_col(self, kind, d):
        slot = self.col_slot(kind % 2, d, kind // 2)
        pltpu.make_async_remote_copy(
            src_ref=slot, dst_ref=slot,
            send_sem=self.col_sems.at[kind, d], recv_sem=self.col_sems.at[kind, d],
            device_id=self.here.along_b(0, 1), device_id_type=MESH,
        ).wait_recv()


def send_part(src, dst, send_sem, recv_sem, target):
    copy = pltpu.make_async_remote_copy(
        src_ref=src,
        dst_ref=dst,
        send_sem=send_sem,
        recv_sem=recv_sem,
        device_id=target,
        device_id_type=MESH,
    )
    copy.start()
    return copy


def scatter_rows(here, group, part, into, send_sems, recv_sems):
    copies = []
    for q in (1, 0):
        for p in reversed(range(HALF)):
            k = ORDER[group * HALF + p]
            if q == 0 and k == 0:
                continue
            at = (q * HALF + p) * OWN * SI
            copies.append(
                send_part(
                    part.at[group, at : at + OWN * SI, :], into.at[q * 8 + k],
                    send_sems.at[q * 8 + k], recv_sems.at[q * 8 + k], here.along_b(q, k),
                )
            )
    return copies


def scatter_cols(here, part, into, send_sems, recv_sems):
    copies = []
    for n in (6, 5, 7, 2, 1, 3, 4):
        target = here.along_a(n // 4, n % 4, 0)
        at = pl.multiple_of(target[0] // 2 * OWN * SI, 8)
        copies.append(
            send_part(
                part.at[pl.ds(at, OWN * SI), :], into.at[n], send_sems.at[n],
                recv_sems.at[n], target,
            )
        )
    return copies


def whole_body(
    t_hbm, g_hbm, h_hbm, q_hbm, r_hbm, u_hbm, ve_hbm, oe_hbm, se_hbm,
    row_out, col_out,
    t_ref, g_in, h_in, q_in, r_in, u_in, ve_ref, oe_ref, se_ref,
    q_ref, amp, rows, cols, a_ref, g2, r2, bdh, bdu, p_ref, c_ref, yr, yc, res, held,
    row_part, col_part, row_into, col_into, twin_into, col_sum,
    in_sems, gather_sems, row_sems, col_sems, out_row_sems, out_col_sems, sum_row_sems,
    sum_col_sems,
):
    here = Place()
    loads = [
        pltpu.make_async_copy(src, dst, in_sems.at[n])
        for n, (src, dst) in enumerate(
            (
                (g_hbm, g_in), (h_hbm, h_in), (r_hbm, r_in), (u_hbm, u_in), (q_hbm, q_in),
                (ve_hbm, ve_ref), (oe_hbm, oe_ref), (se_hbm, se_ref), (t_hbm, t_ref),
            )
        )
    ]
    for load in loads:
        load.start()
    barrier = pltpu.get_barrier_semaphore()
    near = [here.along_b(0, k) for k in range(1, 8)] + [here.along_b(1, 0)]
    near += [here.along_a(0, d, 0) for d in range(1, 4)]
    near += [here.along_a(1, 0, 0), here.along_a(0, 0, 1)]
    for target in near:
        pl.semaphore_signal(barrier, inc=1, device_id=target, device_id_type=MESH)
    for load in loads[:4]:
        load.wait()
    own_col = cols.at[pl.ds(pl.multiple_of(here.a * CHUNK, 16), CHUNK), :]
    split_l(g_in, h_in, r_in, u_in, rows.at[0:CHUNK, :], own_col, amp)
    pl.semaphore_wait(barrier, len(near))
    net = Gather(here, rows, cols, gather_sems, row_sems, col_sems)
    net.across_x(0)
    for k in ORDER:
        if k:
            net.along_z(k)
    net.swap_col()
    net.round_col(0)
    net.twin_col(0, 0)
    for load in loads[4:]:
        load.wait()
    split_q(q_in, q_ref)
    net.got_col(1, 0)
    net.round_col(1)
    net.twin_col(1, 0)
    compute_a(here, t_ref, q_ref, a_ref, 0, 2)
    others = [k for k in ORDER if k]
    for k in others[0:2]:
        net.got_row(0, k)
        net.across_x(k)
    for d in range(1, 4):
        net.got_col(0, d)
        net.twin_col(0, d)
    compute_a(here, t_ref, q_ref, a_ref, 2, 2)
    for k in others[2:4]:
        net.got_row(0, k)
        net.across_x(k)
    for d in range(1, 4):
        net.got_col(1, d)
        net.twin_col(1, d)
    compute_a(here, t_ref, q_ref, a_ref, 4, 2)
    for k in others[4:6]:
        net.got_row(0, k)
        net.across_x(k)
    compute_a(here, t_ref, q_ref, a_ref, 6, 2)
    for k in others[6:]:
        net.got_row(0, k)
        net.across_x(k)
    clear_off(bdh, bdu)
    for kind in (2, 3):
        for d in range(4):
            net.got_col(kind, d)
    spread(cols, functools.partial(put_cols, bdh, bdu))
    base = pair_energy(here, ve_ref)
    row_sums = []
    for group in range(2):
        for k in ORDER[group * HALF : (group + 1) * HALF]:
            net.got_row(1, k)
        spread_rows(group, rows, g2, r2)
        compute_pc(g2, r2, bdh, bdu, p_ref, c_ref)
        for s in range(NC):
            weigh(oe_ref, se_ref, base, group, s, a_ref, p_ref, c_ref, yr, yc)
        row_residual(bdh, yr, res, row_part.at[group])
        row_sums += scatter_rows(
            here, group, row_part, row_into, out_row_sems, sum_row_sems
        )
        turned = g2[...].T
        for s in range(NC):
            if group == 0:
                col_first(s, turned, yc, held)
                continue
            col_residual(s, turned, yc, held, res, col_part)
    twin = send_part(
        col_part.at[1 - here.core], twin_into, out_col_sems.at[0], sum_col_sems.at[0],
        here.along_a(0, 0, 1),
    )
    for copy in net.sent:
        copy.wait_send()
    twin.wait_recv()
    col_sum[...] = col_part[here.core] + twin_into[...]
    col_sums = scatter_cols(here, col_sum, col_into, out_col_sems, sum_col_sems)
    total = col_sum[pl.ds(pl.multiple_of(here.a // 2 * OWN * SI, 8), OWN * SI), :]
    for copy in col_sums:
        copy.wait_recv()
    for n in range(1, 8):
        total = total + col_into[n]
    col_out[...] = total
    at = ORDER.index(0)
    total = row_part[at // HALF, at % HALF * OWN * SI : (at % HALF + 1) * OWN * SI, :]
    for copy in row_sums:
        copy.wait_recv()
    for n in range(1, GROUP):
        total = total + row_into[n]
    row_out[...] = total
    for copy in row_sums + col_sums + [twin]:
        copy.wait_send()


def on_device(
    pair_amplitude,
    row_amplitude,
    column_amplitude,
    row_integral,
    column_integral,
    step_integral,
    virtual_energy,
    occupied_energy,
    step_energy,
):
    factor = 1.0 / (math.sqrt(virtual_energy.shape[0]) * OT)
    t = pair_amplitude.transpose(0, 2, 1, 3)
    r = row_amplitude.transpose(0, 2, 1, 3).reshape(OWN * SI, NO)
    u = column_amplitude.transpose(0, 2, 1, 3).reshape(OWN * SI, NO)
    ve = virtual_energy.reshape(8, NO)
    operands = (
        t, row_integral, column_integral, step_integral, r, u, ve, occupied_energy, step_energy
    )
    out = pltpu.VMEM((NC * USED, NO), F32)
    vm = pl.BlockSpec(memory_space=pltpu.VMEM)
    spaces = [pltpu.VMEM] * 7 + [pltpu.SMEM] * 2
    order = range(9)
    dma = pltpu.SemaphoreType.DMA
    results = pl.pallas_call(
        whole_body,
        out_shape=(out, out),
        in_specs=[pl.BlockSpec(memory_space=pl.ANY)] * 9,
        out_specs=(vm, vm),
        scratch_shapes=[spaces[n](operands[n].shape, operands[n].dtype) for n in order]
        + [
            pltpu.VMEM((64, NO), BF16),
            pltpu.VMEM((2, OWN * SI, NO), F32),
            pltpu.VMEM((GROUP * CHUNK, NO), BF16),
            pltpu.VMEM((GROUP * CHUNK, NO), BF16),
            pltpu.VMEM((32 * OT * AROWS, NO), F32),
            pltpu.VMEM((JK * 16, 2 * NO), BF16),
            pltpu.VMEM((SI * 16, 2 * NO), BF16),
            pltpu.VMEM((JK * NO, 2 * NO), BF16),
            pltpu.VMEM((SI * NO, 2 * NO), BF16),
            pltpu.VMEM((JK * 160, NO), F32),
            pltpu.VMEM((SI * 400, NO), F32),
            pltpu.VMEM((160, JK * NO), BF16),
            pltpu.VMEM((SI * 400, NO), BF16),
            pltpu.VMEM((OT * 64, NO), F32),
            pltpu.VMEM((SI, NO, NO), F32),
            pltpu.VMEM((2, 2 * HALF * OWN * SI, NO), F32),
            pltpu.VMEM((2, 8 * OWN * SI, NO), F32),
            pltpu.VMEM((GROUP, OWN * SI, NO), F32),
            pltpu.VMEM((8, OWN * SI, NO), F32),
            pltpu.VMEM((8 * OWN * SI, NO), F32),
            pltpu.VMEM((8 * OWN * SI, NO), F32),
            dma((9,)),
            dma((30,)),
            dma((2, 8)),
            dma((4, 4)),
            dma((GROUP,)),
            dma((8,)),
            dma((GROUP,)),
            dma((8,)),
        ],
        compiler_params=pltpu.CompilerParams(
            collective_id=0, has_side_effects=True, vmem_limit_bytes=56 * 2**20
        ),
    )(*operands)
    return tuple(
        (x * factor).reshape(OWN, OT, NC, NO).transpose(0, 2, 1, 3) for x in results
    )


def solution(mesh):
    placed = (
        P("aa", "ba", None, None),
        P(("aa", "ba"), None, None, None),
        P(("ba", "aa"), None, None, None),
        P(("aa", "ba"), None),
        P(("ba", "aa"), None),
        P(),
        P(),
        P(),
        P(),
    )
    return jax.shard_map(
        on_device,
        mesh=mesh,
        in_specs=placed,
        out_specs=(P(("aa", "ba"), None, None, None), P(("ba", "aa"), None, None, None)),
        check_vma=False,
    )
```

```python
import functools
import math

import jax
import jax.numpy as jnp
from jax import lax
from jax.experimental import pallas as pl
from jax.experimental.pallas import tpu as pltpu
from jax.sharding import PartitionSpec as P

F32 = jnp.float32
BF16 = jnp.bfloat16
MESH = pl.DeviceIdType.MESH
GROUP = 16
OWN = 4
OT = 5
JK = OT * OT
NC = 2
SI = OT * NC
NO = 128
CHUNK = 144
USED = OWN * OT
ORDER = (0, 1, 7, 2, 6, 3, 5, 4)
HALF = 4
AROWS = 56
NT = (((1,), (1,)), ((), ()))


def dot_nt(x, y):
    return lax.dot_general(x, y, NT, preferred_element_type=F32)


def by_jk(moved, first, stride, count):
    lane = lax.broadcasted_iota(jnp.int32, (8, NO), 1)
    found = []
    for jk in range(JK):
        source = (JK * ((lane - 41 * jk) & 127) + jk) >> 7
        t = moved[first : first + 8]
        for m in range(1, JK):
            at = first + stride * m
            t = jnp.where(source == m, moved[at : at + 8], t)
        shift = (-41 * jk) % 128
        found.append(pltpu.roll(t, shift, 1) if shift else t)
    return found


def permute_lanes(parts):
    row = lax.broadcasted_iota(jnp.int32, (NO, NO), 0)
    col = lax.broadcasted_iota(jnp.int32, (NO, NO), 1)
    perm = (row == ((JK * col) & 127)).astype(F32).astype(BF16)
    stacked = jnp.concatenate(
        [part[:, m * NO : (m + 1) * NO] for m in range(JK) for part in parts], 0
    ).astype(BF16)
    return jnp.dot(stacked, perm, preferred_element_type=F32)


def put_chunk(tables, src, amp, dst):
    amp[...] = src[...].astype(F32)
    pieces = tables + [
        amp[pl.ds(i * NC + s, OWN, stride=SI), :] for s in range(NC) for i in range(OT)
    ]
    pieces.append(jnp.zeros((4, NO), F32))
    for k in range(9):
        dst[16 * k : 16 * k + 16, :] = jnp.concatenate(
            pieces[4 * k : 4 * k + 4], 0
        ).astype(BF16)


def split_q(q_ref, q_out):
    low = jnp.concatenate([q_ref[...].astype(F32), jnp.zeros((6, JK * NO), F32)], 0)
    lows = by_jk(permute_lanes([low]), 0, 8, JK)
    rows = [lows[jk][s : s + 1] for s in range(NC) for jk in range(JK)]
    rows.append(jnp.zeros((64 - NC * JK, NO), F32))
    q_out[...] = jnp.concatenate(rows, 0).astype(BF16)


def split_l(g_ref, h_ref, r_ref, u_ref, row_chunk, col_chunk, amp):
    top = jnp.concatenate([g_ref[...].astype(F32), h_ref[...].astype(F32)], 0)
    tops = by_jk(permute_lanes([top]), 0, 8, JK)
    put_chunk([t[0:4] for t in tops], r_ref, amp.at[0], row_chunk)
    put_chunk([t[4:8] for t in tops], u_ref, amp.at[1], col_chunk)


class Place:
    def __init__(self):
        self.a = lax.axis_index("aa")
        self.b = lax.axis_index("ba")
        self.core = lax.rem(self.a, 2)
        self.y = lax.rem(self.a // 2, 4)
        self.xl = self.a // 8
        self.xh = self.b // 8
        self.z = lax.rem(self.b, 8)

    def index_b(self, q, k):
        xh = 1 - self.xh if q else self.xh
        return xh * 8 + lax.rem(self.z - k + 8, 8)

    def along_b(self, q, k):
        return (self.a, self.index_b(q, k))

    def index_a(self, q, d, c):
        xl = 1 - self.xl if q else self.xl
        core = 1 - self.core if c else self.core
        return (xl * 4 + lax.rem(self.y - d + 4, 4)) * 2 + core

    def along_a(self, q, d, c):
        return (self.index_a(q, d, c), self.b)


def compute_a(here, t_ref, q_ref, a_out, first, count):
    q = q_ref[0:AROWS, :]
    for at_k in range(first, first + count):
        zk = lax.rem(here.z - ORDER[at_k] + 8, 8)
        near_k = (here.xh * 8 + zk) * OWN
        far_k = ((1 - here.xh) * 8 + zk) * OWN

        def pair(n, _, at_k=at_k, near_k=near_k, far_k=far_k):
            near, far = near_k + 2 * n, far_k + 2 * n
            for i in range(OT):
                block = jnp.concatenate(
                    [t_ref[near, i], t_ref[far, i], t_ref[near + 1, i], t_ref[far + 1, i]],
                    0,
                )
                part = dot_nt(q, block)
                for half in range(2):
                    at = pl.multiple_of(
                        (4 * at_k + 2 * n + half) * (OT * AROWS) + i * AROWS, 8
                    )
                    a_out[pl.ds(at, AROWS), :] = part[:, half * NO : (half + 1) * NO]
            return 0

        lax.fori_loop(0, 2, pair, 0)


def pair_energy(here, ve_ref):
    lane = lax.broadcasted_iota(jnp.int32, (32, NO), 1)
    row = lax.broadcasted_iota(jnp.int32, (32, NO), 0)
    offset = jnp.zeros((32, NO), jnp.int32)
    for at_k, k in enumerate(ORDER):
        offset = jnp.where((row >> 2) == at_k, k, offset)
    zk = (here.z - offset) & 7
    lead = jnp.broadcast_to(ve_ref[pl.ds(here.a // 2, 1), :], (32, NO))
    first = lax.rem(here.a, 2) * 64
    halves = []
    for xh in (here.xh, 1 - here.xh):
        at = first + (xh * 8 + zk) * OWN + (row & 3)
        halves.append(jnp.sum(jnp.where(lane == at, lead, 0.0), 1, keepdims=True))
    tail = ve_ref[pl.ds(here.b // 2, 1), :]
    turned = pltpu.roll(jnp.broadcast_to(tail, (8, NO)), 64, 1)[0:1]
    keep = (lane[0:1] // 64) == lax.rem(here.b, 2)
    tail = jnp.where(keep, tail, turned)
    return jnp.where(lane < 64, halves[0], halves[1]) + tail


def spread(src, wide):
    for k in range(9):
        blocks = [
            src[e * CHUNK + 16 * k : e * CHUNK + 16 * k + 16, :].astype(F32)
            for e in range(GROUP)
        ]
        for c in range(4):
            at = 4 * k + c
            if at >= JK + SI:
                continue
            tile = jnp.concatenate([b[4 * c : 4 * c + 4] for b in blocks], 0)
            wide(at, tile.astype(BF16))


def spread_rows(group, rows, g2, r2):
    for k in range(9):
        for q in range(2):
            blocks = []
            for offset in ORDER[group * HALF : (group + 1) * HALF]:
                at = (q * 8 + offset) * CHUNK + 16 * k
                blocks.append(rows[at : at + 16, :].astype(F32))
            for c in range(4):
                at = 4 * k + c
                if at >= JK + SI:
                    continue
                tile = jnp.concatenate([b[4 * c : 4 * c + 4] for b in blocks], 0)
                dst, to = (g2, at) if at < JK else (r2, at - JK)
                dst[to * 16 : to * 16 + 16, q * NO : (q + 1) * NO] = tile.astype(BF16)


def put_cols(bdh, bdu, at, tile):
    dst, c = (bdh, at) if at < JK else (bdu, at - JK)
    dst[c * NO : c * NO + 64, 0:NO] = tile
    dst[c * NO + 64 : c * NO + NO, NO : 2 * NO] = tile


def clear_off(bdh, bdu):
    zero = jnp.zeros((64, NO), BF16)
    for dst, count in ((bdh, JK), (bdu, SI)):
        for c in range(count):
            dst[c * NO : c * NO + 64, NO : 2 * NO] = zero
            dst[c * NO + 64 : c * NO + NO, 0:NO] = zero


def compute_pc(g2, r2, bdh, bdu, p_out, c_out):
    r = r2[...]
    for n in range(JK // 2 + 1):
        width = 2 if n < JK // 2 else 1
        part = dot_nt(r, bdh[2 * n * NO : (2 * n + width) * NO, :])
        for half in range(width):
            p_out[(2 * n + half) * 160 : (2 * n + half + 1) * 160, :] = part[
                :, half * NO : (half + 1) * NO
            ]
    for n in range(OT):
        part = dot_nt(g2[...], bdu[2 * n * NO : (2 * n + 2) * NO, :])
        for half in range(2):
            at = (2 * n + half) * 400
            c_out[at : at + 400, :] = part[:, half * NO : (half + 1) * NO]


def cycles():
    found, seen = [], set()
    for n in range(OT**3):
        i, j, k = n // JK, n // OT % OT, n % OT
        if (i, j, k) not in seen:
            turns = [(i, j, k), (j, k, i), (k, i, j)]
            found.append(turns if i != j or j != k else turns[:1])
            seen.update(turns)
    return found


def weigh(oe_ref, se_ref, base, group, s, a_in, p_in, c_in, yr, yc):
    start = base[group * 16 : group * 16 + 16] + se_ref[s]
    first = group * 16 * OT * AROWS + s * JK
    for turns in cycles():
        i, j, k = turns[0]
        inverse = 1.0 / (start - ((oe_ref[i] + oe_ref[j]) + oe_ref[k]))
        a, p, c = [], [], []
        for x, y, z in turns:
            yz = y * OT + z
            at = first + x * AROWS + yz
            a.append(a_in[pl.ds(at, 16, stride=OT * AROWS), :])
            at = yz * 160 + (s * OT + x) * 16
            p.append(p_in[at : at + 16, :])
            at = (s * OT + x) * 400 + yz * 16
            c.append(c_in[at : at + 16, :])
        count = len(turns)
        for n, (x, y, z) in enumerate(turns):
            one, two = (n + 1) % count, (n + 2) % count
            w = (a[n] + a[one]) + (p[n] + p[two]) + (c[one] + c[two])
            out = (w * inverse).astype(BF16)
            yz = y * OT + z
            at = (s * OT + x) * 16
            yr[at : at + 16, yz * NO : (yz + 1) * NO] = out
            at = (s * OT + y) * 400 + (z * OT + x) * 16
            yc[at : at + 16, :] = out


def row_residual(bdh, yr, res, row_out):
    out = jnp.dot(yr[...], bdh[...], preferred_element_type=F32)
    for c in range(SI):
        for q in range(2):
            res[c * 32 + q * 16 : c * 32 + q * 16 + 16, :] = out[
                c * 16 : c * 16 + 16, q * NO : (q + 1) * NO
            ]
    for c in range(SI):
        for v in range(OWN):
            at = v * SI + c % OT * NC + c // OT
            row_out[pl.ds(at, 2 * HALF, stride=OWN * SI), :] = res[
                pl.ds(c * 32 + v, 2 * HALF, stride=OWN), :
            ]


def col_products(s, turned, yc):
    lane = lax.broadcasted_iota(jnp.int32, (NO, NO), 1)
    moved = jnp.concatenate(
        [yc[(s * OT + j) * 400 : (s * OT + j + 1) * 400, :] for j in range(OT)], 1
    )
    out = jnp.dot(turned, moved, preferred_element_type=F32)
    pieces = [out[:, j * NO : (j + 1) * NO] for j in range(OT)]
    return [jnp.where(lane < 64, piece[0:NO], piece[NO:]) for piece in pieces]


def col_first(s, turned, yc, held):
    for j, piece in enumerate(col_products(s, turned, yc)):
        held[s * OT + j] = piece


def col_residual(s, turned, yc, held, res, col_out):
    for j, piece in enumerate(col_products(s, turned, yc)):
        both = (piece + held[s * OT + j]).T
        res[j * 64 : j * 64 + 64, :] = both[0:64] + both[64:128]
    for j in range(OT):
        for core in range(2):
            for v in range(OWN):
                col_out[core, pl.ds(v * SI + j * NC + s, 8, stride=OWN * SI), :] = res[
                    pl.ds(j * 64 + core * OWN + v, 8, stride=2 * OWN), :
                ]


class Gather:
    def __init__(self, here, rows, cols, send_sems, row_sems, col_sems):
        self.here, self.rows, self.cols = here, rows, cols
        self.send_sems, self.row_sems, self.col_sems = send_sems, row_sems, col_sems
        self.sent = []

    def copy(self, src, dst, recv_sem, target):
        copy = pltpu.make_async_remote_copy(
            src_ref=src,
            dst_ref=dst,
            send_sem=self.send_sems.at[len(self.sent)],
            recv_sem=recv_sem,
            device_id=target,
            device_id_type=MESH,
        )
        copy.start()
        self.sent.append(copy)

    def row_slot(self, q, k):
        at = (q * 8 + k) * CHUNK
        return self.rows.at[at : at + CHUNK, :]

    def col_slot(self, q, d, c):
        at = pl.multiple_of(self.here.index_a(q, d, c) * CHUNK, 16)
        return self.cols.at[pl.ds(at, CHUNK), :]

    def along_z(self, k):
        self.copy(
            self.row_slot(0, 0), self.row_slot(0, k), self.row_sems.at[0, k],
            self.here.along_b(0, -k),
        )

    def across_x(self, k):
        self.copy(
            self.row_slot(0, k), self.row_slot(1, k), self.row_sems.at[1, k],
            self.here.along_b(1, 0),
        )

    def got_row(self, q, k):
        pltpu.make_async_remote_copy(
            src_ref=self.row_slot(q, k), dst_ref=self.row_slot(q, k),
            send_sem=self.row_sems.at[q, k], recv_sem=self.row_sems.at[q, k],
            device_id=self.here.along_b(0, 1), device_id_type=MESH,
        ).wait_recv()

    def col_to(self, q, d, c, kind, step, target):
        slot = self.col_slot(q, d, c)
        self.copy(slot, slot, self.col_sems.at[kind, step], target)

    def swap_col(self):
        self.col_to(0, 0, 0, 1, 0, self.here.along_a(1, 0, 0))

    def round_col(self, q):
        for d in range(1, 4):
            self.col_to(q, 0, 0, q, d, self.here.along_a(0, -d, 0))

    def twin_col(self, q, d):
        self.col_to(q, d, 0, 2 + q, d, self.here.along_a(0, 0, 1))

    def got_col(self, kind, d):
        slot = self.col_slot(kind % 2, d, kind // 2)
        pltpu.make_async_remote_copy(
            src_ref=slot, dst_ref=slot,
            send_sem=self.col_sems.at[kind, d], recv_sem=self.col_sems.at[kind, d],
            device_id=self.here.along_b(0, 1), device_id_type=MESH,
        ).wait_recv()


def send_part(src, dst, send_sem, recv_sem, target):
    copy = pltpu.make_async_remote_copy(
        src_ref=src,
        dst_ref=dst,
        send_sem=send_sem,
        recv_sem=recv_sem,
        device_id=target,
        device_id_type=MESH,
    )
    copy.start()
    return copy


def scatter_rows(here, group, part, into, send_sems, recv_sems):
    copies = []
    for q in (1, 0):
        for p in reversed(range(HALF)):
            k = ORDER[group * HALF + p]
            if q == 0 and k == 0:
                continue
            at = (q * HALF + p) * OWN * SI
            copies.append(
                send_part(
                    part.at[group, at : at + OWN * SI, :], into.at[q * 8 + k],
                    send_sems.at[q * 8 + k], recv_sems.at[q * 8 + k], here.along_b(q, k),
                )
            )
    return copies


def scatter_cols(here, part, into, send_sems, recv_sems):
    copies = []
    for n in (6, 5, 7, 2, 1, 3, 4):
        target = here.along_a(n // 4, n % 4, 0)
        at = pl.multiple_of(target[0] // 2 * OWN * SI, 8)
        copies.append(
            send_part(
                part.at[pl.ds(at, OWN * SI), :], into.at[n], send_sems.at[n],
                recv_sems.at[n], target,
            )
        )
    return copies


def whole_body(
    t_hbm, g_hbm, h_hbm, q_hbm, r_hbm, u_hbm, ve_hbm, oe_hbm, se_hbm,
    row_out, col_out,
    t_ref, g_in, h_in, q_in, r_in, u_in, ve_ref, oe_ref, se_ref,
    q_ref, amp, rows, cols, a_ref, g2, r2, bdh, bdu, p_ref, c_ref, yr, yc, res, held,
    row_part, col_part, row_into, col_into, twin_into, col_sum,
    in_sems, gather_sems, row_sems, col_sems, out_row_sems, out_col_sems, sum_row_sems,
    sum_col_sems,
):
    here = Place()
    loads = [
        pltpu.make_async_copy(src, dst, in_sems.at[n])
        for n, (src, dst) in enumerate(
            (
                (g_hbm, g_in), (h_hbm, h_in), (r_hbm, r_in), (u_hbm, u_in), (q_hbm, q_in),
                (ve_hbm, ve_ref), (oe_hbm, oe_ref), (se_hbm, se_ref), (t_hbm, t_ref),
            )
        )
    ]
    for load in loads:
        load.start()
    barrier = pltpu.get_barrier_semaphore()
    near = [here.along_b(0, k) for k in range(1, 8)] + [here.along_b(1, 0)]
    near += [here.along_a(0, d, 0) for d in range(1, 4)]
    near += [here.along_a(1, 0, 0), here.along_a(0, 0, 1)]
    for target in near:
        pl.semaphore_signal(barrier, inc=1, device_id=target, device_id_type=MESH)
    for load in loads[:4]:
        load.wait()
    own_col = cols.at[pl.ds(pl.multiple_of(here.a * CHUNK, 16), CHUNK), :]
    split_l(g_in, h_in, r_in, u_in, rows.at[0:CHUNK, :], own_col, amp)
    pl.semaphore_wait(barrier, len(near))
    net = Gather(here, rows, cols, gather_sems, row_sems, col_sems)
    net.across_x(0)
    for k in ORDER:
        if k:
            net.along_z(k)
    net.swap_col()
    net.round_col(0)
    net.twin_col(0, 0)
    for load in loads[4:]:
        load.wait()
    split_q(q_in, q_ref)
    net.got_col(1, 0)
    net.round_col(1)
    net.twin_col(1, 0)
    compute_a(here, t_ref, q_ref, a_ref, 0, 2)
    others = [k for k in ORDER if k]
    for k in others[0:2]:
        net.got_row(0, k)
        net.across_x(k)
    for d in range(1, 4):
        net.got_col(0, d)
        net.twin_col(0, d)
    compute_a(here, t_ref, q_ref, a_ref, 2, 1)
    for k in others[2:4]:
        net.got_row(0, k)
        net.across_x(k)
    for d in range(1, 4):
        net.got_col(1, d)
        net.twin_col(1, d)
    compute_a(here, t_ref, q_ref, a_ref, 3, 1)
    for k in others[4:6]:
        net.got_row(0, k)
        net.across_x(k)
    compute_a(here, t_ref, q_ref, a_ref, 4, 1)
    for k in others[6:]:
        net.got_row(0, k)
        net.across_x(k)
    compute_a(here, t_ref, q_ref, a_ref, 5, 3)
    clear_off(bdh, bdu)
    for kind in (2, 3):
        for d in range(4):
            net.got_col(kind, d)
    spread(cols, functools.partial(put_cols, bdh, bdu))
    base = pair_energy(here, ve_ref)
    row_sums = []
    for group in range(2):
        for k in ORDER[group * HALF : (group + 1) * HALF]:
            net.got_row(1, k)
        spread_rows(group, rows, g2, r2)
        compute_pc(g2, r2, bdh, bdu, p_ref, c_ref)
        for s in range(NC):
            weigh(oe_ref, se_ref, base, group, s, a_ref, p_ref, c_ref, yr, yc)
        row_residual(bdh, yr, res, row_part.at[group])
        row_sums += scatter_rows(
            here, group, row_part, row_into, out_row_sems, sum_row_sems
        )
        turned = g2[...].T
        for s in range(NC):
            if group == 0:
                col_first(s, turned, yc, held)
                continue
            col_residual(s, turned, yc, held, res, col_part)
    twin = send_part(
        col_part.at[1 - here.core], twin_into, out_col_sems.at[0], sum_col_sems.at[0],
        here.along_a(0, 0, 1),
    )
    for copy in net.sent:
        copy.wait_send()
    twin.wait_recv()
    col_sum[...] = col_part[here.core] + twin_into[...]
    col_sums = scatter_cols(here, col_sum, col_into, out_col_sems, sum_col_sems)
    total = col_sum[pl.ds(pl.multiple_of(here.a // 2 * OWN * SI, 8), OWN * SI), :]
    for copy in col_sums:
        copy.wait_recv()
    for n in range(1, 8):
        total = total + col_into[n]
    col_out[...] = total
    at = ORDER.index(0)
    total = row_part[at // HALF, at % HALF * OWN * SI : (at % HALF + 1) * OWN * SI, :]
    for copy in row_sums:
        copy.wait_recv()
    for n in range(1, GROUP):
        total = total + row_into[n]
    row_out[...] = total
    for copy in row_sums + col_sums + [twin]:
        copy.wait_send()


def on_device(
    pair_amplitude,
    row_amplitude,
    column_amplitude,
    row_integral,
    column_integral,
    step_integral,
    virtual_energy,
    occupied_energy,
    step_energy,
):
    factor = 1.0 / (math.sqrt(virtual_energy.shape[0]) * OT)
    t = pair_amplitude.transpose(0, 2, 1, 3)
    r = row_amplitude.transpose(0, 2, 1, 3).reshape(OWN * SI, NO)
    u = column_amplitude.transpose(0, 2, 1, 3).reshape(OWN * SI, NO)
    ve = virtual_energy.reshape(8, NO)
    operands = (
        t, row_integral, column_integral, step_integral, r, u, ve, occupied_energy, step_energy
    )
    out = pltpu.VMEM((NC * USED, NO), F32)
    vm = pl.BlockSpec(memory_space=pltpu.VMEM)
    spaces = [pltpu.VMEM] * 7 + [pltpu.SMEM] * 2
    order = range(9)
    dma = pltpu.SemaphoreType.DMA
    results = pl.pallas_call(
        whole_body,
        out_shape=(out, out),
        in_specs=[pl.BlockSpec(memory_space=pl.ANY)] * 9,
        out_specs=(vm, vm),
        scratch_shapes=[spaces[n](operands[n].shape, operands[n].dtype) for n in order]
        + [
            pltpu.VMEM((64, NO), BF16),
            pltpu.VMEM((2, OWN * SI, NO), F32),
            pltpu.VMEM((GROUP * CHUNK, NO), BF16),
            pltpu.VMEM((GROUP * CHUNK, NO), BF16),
            pltpu.VMEM((32 * OT * AROWS, NO), F32),
            pltpu.VMEM((JK * 16, 2 * NO), BF16),
            pltpu.VMEM((SI * 16, 2 * NO), BF16),
            pltpu.VMEM((JK * NO, 2 * NO), BF16),
            pltpu.VMEM((SI * NO, 2 * NO), BF16),
            pltpu.VMEM((JK * 160, NO), F32),
            pltpu.VMEM((SI * 400, NO), F32),
            pltpu.VMEM((160, JK * NO), BF16),
            pltpu.VMEM((SI * 400, NO), BF16),
            pltpu.VMEM((OT * 64, NO), F32),
            pltpu.VMEM((SI, NO, NO), F32),
            pltpu.VMEM((2, 2 * HALF * OWN * SI, NO), F32),
            pltpu.VMEM((2, 8 * OWN * SI, NO), F32),
            pltpu.VMEM((GROUP, OWN * SI, NO), F32),
            pltpu.VMEM((8, OWN * SI, NO), F32),
            pltpu.VMEM((8 * OWN * SI, NO), F32),
            pltpu.VMEM((8 * OWN * SI, NO), F32),
            dma((9,)),
            dma((30,)),
            dma((2, 8)),
            dma((4, 4)),
            dma((GROUP,)),
            dma((8,)),
            dma((GROUP,)),
            dma((8,)),
        ],
        compiler_params=pltpu.CompilerParams(
            collective_id=0, has_side_effects=True, vmem_limit_bytes=56 * 2**20
        ),
    )(*operands)
    return tuple(
        (x * factor).reshape(OWN, OT, NC, NO).transpose(0, 2, 1, 3) for x in results
    )


def solution(mesh):
    placed = (
        P("aa", "ba", None, None),
        P(("aa", "ba"), None, None, None),
        P(("ba", "aa"), None, None, None),
        P(("aa", "ba"), None),
        P(("ba", "aa"), None),
        P(),
        P(),
        P(),
        P(),
    )
    return jax.shard_map(
        on_device,
        mesh=mesh,
        in_specs=placed,
        out_specs=(P(("aa", "ba"), None, None, None), P(("ba", "aa"), None, None, None)),
        check_vma=False,
    )
```
